256 devices in a mesh: section: 8 (over z_hi, x), dp: 32 (over z_lo, y, core).
Axes of the slice: x: 4, y: 4, z: 8 (z_hi: 2, z_lo: 4; z = z_hi * 4 + z_lo), core: 2. Of those that a mesh axis runs over, the one named last changes fastest.
Arguments:
- inputs: bfloat16 [32, 128, 8192], P(None, 'dp'), may hold values from -16 to 16
- layer_gain: float32 [8, 8192], P('section'), may hold values from 0.5 to 1.5
- layer_down: bfloat16 [8, 8192, 128], P('section', 'dp'), may hold values from -0.0625 to 0.0625
- layer_up: bfloat16 [8, 128, 8192], P('section', None, 'dp'), may hold values from -0.5 to 0.5
- exit_norm_gain: float32 [8192], replicated, may hold values from 0.5 to 1.5
- head_weight: bfloat16 [8192, 16384], P('section', 'dp'), may hold values from -0.1875 to 0.1875
- targets: int32 [32, 128], replicated, may hold values from 0 to 16383
- exit_section: int32 [32], replicated, may hold values from 0 to 7, as said below
Outputs:
- exit_loss: float32 [8, 4, 128], P('section', None, 'dp')
The draws below stay inside these ranges and needn't reach their ends.
Inputs may be any that keep to these rules, and one draw needn't show every extreme that they name: `exit_section`: each of the 8 sections is the exit of exactly 4 micro-batches.
All inputs are finite; a program needn't handle non-finite values.
Results may differ from the reference program's by a relative error of at most 0.0044.
Values may be sent and summed in bfloat16 or wider, within the bound.
No kernel may reach another device: no remote copies, remote signals or barrier semaphores. Data moves between devices by JAX's collectives and lax.ppermute only.
A program may use at most 128 MiB of HBM per device.

```python
import math
import jax
import jax.numpy as jnp
import numpy as np
from jax import lax

D = 8192
V = 16384
R = 128
EXITS = 4
MICRO = 32
TOKENS = 128
N_SECTION = 8


def draw_inputs(key, part):
    key = jax.random.fold_in(key, 11)
    key_base, key_rows, key_cols = jax.random.split(key, 3)
    shape = (MICRO, TOKENS, D)
    row_scale = jnp.exp(jax.random.uniform(key_rows, (MICRO, TOKENS, 1), jnp.float32) * math.log(10.0)) / 3.0
    col_scale = jnp.exp(jax.random.uniform(key_cols, (1, 1, D), jnp.float32, -1.0, 1.0) * math.log(10.0) / 2.0)
    base = jax.random.normal(key_base, shape, jnp.float32)
    return jnp.clip(base * row_scale * col_scale, -16.0, 16.0).astype(jnp.bfloat16)


def draw_exit_section(key, part):
    key = jax.random.fold_in(key, 23)
    listed = (jnp.arange(MICRO, dtype=jnp.int32) % N_SECTION).astype(jnp.int32)
    return jax.random.permutation(key, listed).astype(jnp.int32)


def with_ends(array, stream_key, low, top_value):
    longest = array.shape.index(max(array.shape))
    spots = []
    for shift in (0, 1):
        where = [jax.random.randint(jax.random.fold_in(stream_key, axis), (), 0, length) for axis, length in enumerate(array.shape)]
        where[longest] = (where[longest] + shift) % array.shape[longest]
        spots.append(tuple(where))
    return array.at[spots[0]].set(low).at[spots[1]].set(top_value)


def shard_levels(key, extent, pieces, smallest, high):
    factor_of, own = 1.0, jax.random.fold_in(key, 6)
    for dim, shards_of in pieces:
        draws = jnp.exp(jax.random.uniform(jax.random.fold_in(own, dim), (shards_of,), jnp.float32, smallest / len(pieces), high / len(pieces)))
        factor_of = factor_of * jnp.repeat(draws, extent[dim] // shards_of).reshape([-1 if axis == dim else 1 for axis in range(len(extent))])
    return factor_of


def cumulative_ranks(amount, lean):
    weights = [(1 << 20) // math.isqrt(rank ** lean) + 1 for rank in range(1, amount + 1)]
    deviation = 1 + sum(weights) // (1 << 30)
    return np.cumsum(np.array([max(1, weight // deviation) for weight in weights]))


def ranked_ids(stream_key, shape, number_of, lean):
    grid = cumulative_ranks(number_of, lean)
    pick = jax.random.randint(jax.random.fold_in(stream_key, 1), shape, 0, int(grid[number_of - 1]))
    rank = jnp.searchsorted(jnp.asarray(grid, jnp.int32), pick, side="right")
    return jax.random.permutation(jax.random.fold_in(stream_key, 2), number_of)[rank].astype(jnp.int32)


def centred(rng, shape, deviation, bound, shards=(), held_as=jnp.bfloat16):
    drawn = jax.random.normal(rng, shape, jnp.float32) * deviation
    if len(shards) > 0:
        drawn = shard_levels(rng, shape, shards, -0.22, 0.18) * drawn
    return jnp.clip(drawn, min=-bound, max=bound).astype(held_as)


def setup_inputs(seed: int = 0) -> dict:
    arg_keys = jax.random.split(jax.random.key(seed), 9)
    inputs = draw_inputs(jax.random.fold_in(arg_keys[8], 71), 0)
    layer_gain = jnp.clip(1.0 + 0.1 * jax.random.normal(arg_keys[1], (N_SECTION, D), jnp.float32), 0.5, 1.5)
    layer_down = centred(arg_keys[2], (N_SECTION, D, R), D ** -0.5, 0.0625, ((0, 8), (1, 32)))
    layer_up = centred(arg_keys[3], (N_SECTION, R, D), R ** -0.5, 0.5, ((0, 8), (2, 32)))
    exit_norm_gain = jnp.clip(1.0 + 0.1 * jax.random.normal(arg_keys[4], (D,), jnp.float32), 0.5, 1.5)
    head_weight = centred(arg_keys[5], (D, V), (D // 9) ** -0.5, 0.1875, ((0, 8), (1, 32)))
    targets = with_ends(ranked_ids(arg_keys[6], (MICRO, TOKENS), V, 2), jax.random.fold_in(arg_keys[6], 3), 0, V - 1).astype(jnp.int32)
    exit_section = draw_exit_section(jax.random.fold_in(arg_keys[8], 71), 0)
    return dict(inputs=inputs, layer_gain=layer_gain, layer_down=layer_down, layer_up=layer_up, exit_norm_gain=exit_norm_gain, head_weight=head_weight, targets=targets, exit_section=exit_section)


EPSILON = 1e-05
LOGIT_CEILING = 30.0
RECIPROCAL_HEAT = 1.0 / 0.7

def normalize(values, gain):
    widened = values.astype(jnp.float32)
    scale = lax.rsqrt(lax.optimization_barrier(jnp.mean(widened * widened, -1, keepdims=True)) + EPSILON)
    return widened * scale * gain.astype(jnp.float32)

def apply_layer(state, gain, down, upward):
    normed = normalize(state, gain).astype(jnp.bfloat16)
    latent = jax.nn.silu(jnp.dot(normed, down, preferred_element_type=jnp.float32)).astype(jnp.bfloat16)
    branch_path = jnp.dot(latent, upward, preferred_element_type=jnp.float32)
    return (state.astype(jnp.float32) + branch_path).astype(jnp.bfloat16)

def token_loss(exit_in, head_weight, target):
    score_logits = jnp.dot(exit_in, head_weight, preferred_element_type=jnp.float32)
    ceiling_logits = LOGIT_CEILING * jnp.tanh(score_logits * RECIPROCAL_HEAT / LOGIT_CEILING)
    exp_total = lax.optimization_barrier(jnp.sum(jnp.exp(ceiling_logits), -1))
    picked = jnp.take_along_axis(ceiling_logits, target[:, None].astype(jnp.int32), 1)[:, 0]
    return jnp.log(exp_total) - picked

def reference(inputs, layer_gain, layer_down, layer_up, exit_norm_gain, head_weight, targets, exit_section):
    order = jnp.arange(MICRO, dtype=jnp.int32)
    same = exit_section[:, None] == exit_section[None, :]
    earlier = order[:, None] > order[None, :]
    ranks = lax.optimization_barrier(jnp.sum((same & earlier).astype(jnp.int32), 1)).astype(jnp.int32)
    losses = []
    for micro in range(MICRO):
        state = inputs[micro]
        kept_state = jnp.zeros_like(state)
        for layer_number in range(N_SECTION):
            state = apply_layer(state, layer_gain[layer_number], layer_down[layer_number], layer_up[layer_number])
            kept_state = jnp.where(exit_section[micro] == layer_number, state, kept_state)
        exit_in = normalize(kept_state, exit_norm_gain).astype(jnp.bfloat16)
        losses.append(token_loss(exit_in, head_weight, targets[micro]))
    stacked = jnp.stack(losses)
    return jnp.zeros((N_SECTION, EXITS, TOKENS), jnp.float32).at[exit_section, ranks].set(stacked)
```

```python
import jax
import jax.numpy as jnp
from jax import lax
from jax.experimental import pallas as pl
from jax.experimental.pallas import tpu as pltpu
from jax.sharding import Mesh, PartitionSpec as P

EPSILON = 1e-05
LOGIT_CEILING = 30.0
RECIPROCAL_HEAT = 1.0 / 0.7
INTERPRET = False

SECTION = ("zhi", "x")
DP = ("zlo", "y", "core")
PLANE = ("zlo", "y")


def spread(block, axis):
    size = lax.axis_size(axis)
    copies = jnp.broadcast_to(block[None], (size, *block.shape))
    return lax.all_to_all(copies, axis, 0, 0, tiled=True)


def swapped(block):
    return lax.ppermute(block, "core", [(0, 1), (1, 0)])


def both_cores(block, axis):
    other = swapped(block)
    first = lax.axis_index("core") == 0
    low = jnp.where(first, block, other)
    high = jnp.where(first, other, block)
    return jnp.stack([low, high]) if axis is None else jnp.concatenate([low, high], axis)


def chain_kernel(exit_ref, products_ref, gram_ref, square_ref, latent_ref, scale_ref):
    layers, _, twice = products_ref.shape
    rank = twice // 2
    width = exit_ref[1].astype(jnp.float32)
    square = square_ref[...]
    for layer in range(layers):
        here = slice(layer * rank, (layer + 1) * rank)
        before = slice(0, layer * rank)
        entering = products_ref[layer, :, :rank]
        cross = products_ref[layer, :, rank:]
        if layer > 0:
            earlier = latent_ref[:, before]
            entering += jnp.dot(earlier, gram_ref[before, here], preferred_element_type=jnp.float32)
            cross += lax.dot_general(
                earlier,
                gram_ref[here, before],
                (((1,), (1,)), ((), ())),
                preferred_element_type=jnp.float32,
            )
        value = entering * lax.rsqrt(square / width + EPSILON)
        latent = (value / (1.0 + jnp.exp(-value))).astype(jnp.bfloat16)
        latent = jnp.where(layer <= exit_ref[0], latent, jnp.zeros_like(latent))
        latent_ref[:, here] = latent
        own = jnp.dot(latent, gram_ref[here, here], preferred_element_type=jnp.float32)
        grown = latent.astype(jnp.float32) * (2.0 * cross + own)
        square = jnp.maximum(square + jnp.sum(grown, -1, keepdims=True), 0.0)
    scale_ref[...] = lax.rsqrt(square / width + EPSILON)


def run_chain(numbers, products, gram, square):
    layers, rows, twice = products.shape
    whole = pl.BlockSpec(memory_space=pltpu.VMEM)
    return pl.pallas_call(
        chain_kernel,
        out_shape=(
            jax.ShapeDtypeStruct((rows, layers * twice // 2), jnp.bfloat16),
            jax.ShapeDtypeStruct((rows, 1), jnp.float32),
        ),
        in_specs=[pl.BlockSpec(memory_space=pltpu.SMEM), whole, whole, whole],
        out_specs=(whole, whole),
        compiler_params=pltpu.CompilerParams(vmem_limit_bytes=16 * 2**20),
        interpret=INTERPRET,
    )(numbers, products, gram, square)


def per_device(
    inputs, layer_gain, layer_down, layer_up, exit_norm_gain, head_weight, targets, exit_section
):
    f32, bf16 = jnp.float32, jnp.bfloat16
    section = lax.axis_index(SECTION)
    place = lax.axis_index(DP)
    micro, tokens, width = inputs.shape
    sections = lax.axis_size(SECTION)
    plane = lax.axis_size(PLANE)
    rank = layer_up.shape[1]
    own_rank = rank // lax.axis_size(DP)
    exits = micro // sections
    rows = exits * tokens
    head_rows, head_columns = head_weight.shape

    order = jnp.arange(micro, dtype=jnp.int32)
    same = exit_section[:, None] == exit_section[None, :]
    ranks = jnp.sum((same & (order[:, None] > order[None, :])).astype(jnp.int32), 1)
    slot = exit_section * exits + ranks
    chosen = jnp.sum(jnp.where(slot[None, :] == order[:, None], order[None, :], 0), 1)

    down = layer_down[0]
    up = layer_up[0]
    features = down.shape[0]
    gain = lax.dynamic_slice_in_dim(layer_gain[0], place * features, features, 0)
    scaled_down = (down.astype(f32) * gain[:, None]).astype(bf16)
    sent = up.reshape(2, 4, 4, own_rank, features).transpose(2, 1, 0, 3, 4)
    sent = sent.reshape(-1, own_rank, features)
    came = lax.all_to_all(sent, DP, 0, 0, tiled=True)
    up_rows = came.transpose(1, 0, 2).reshape(own_rank, width)
    up_rows = spread(up_rows, SECTION)
    pair = jnp.concatenate([scaled_down, up.T], 1)
    gathered = both_cores(spread(spread(pair, "zlo"), "y"), None)
    maps = gathered.transpose(2, 1, 0, 3, 4).reshape(width, 2 * rank)

    wide = inputs.astype(f32)
    squares = jnp.sum(wide * wide, -1)
    flat = jnp.concatenate(
        [inputs.reshape(micro * tokens, width), up_rows.reshape(sections * own_rank, width)], 0
    )
    products = jnp.dot(flat, maps, preferred_element_type=f32)
    state_part = jnp.take(products[: micro * tokens].reshape(micro, tokens, -1), chosen, axis=0)
    state_part = state_part.reshape(sections, rows, 2, rank).transpose(0, 2, 1, 3)
    gram_part = products[micro * tokens :].reshape(sections, own_rank, 2 * rank)
    ahead = (jnp.arange(sections, dtype=jnp.int32) < section)[:, None, None]
    gram_part = jnp.where(ahead, gram_part[..., :rank], gram_part[..., rank:])
    gram_part = gram_part.reshape(sections * own_rank, rank)
    outgoing = jnp.concatenate(
        [
            state_part.reshape(sections, 2 * rows, rank),
            jnp.broadcast_to(gram_part[None], (sections, *gram_part.shape)),
        ],
        1,
    )
    incoming = lax.all_to_all(outgoing, SECTION, 0, 0, tiled=True)
    own_products = incoming[:, : 2 * rows].reshape(sections, 2, rows, rank)
    own_products = own_products.transpose(0, 2, 1, 3).reshape(sections, rows, 2 * rank)
    gram_rows = incoming[:, 2 * rows :].transpose(1, 0, 2).astype(bf16)
    gram_rows = gram_rows.reshape(sections, own_rank, sections * rank)
    gram = both_cores(spread(spread(gram_rows, "zlo"), "y"), None)
    gram = gram.transpose(3, 0, 1, 2, 4, 5).reshape(sections * rank, sections * rank)
    own_micro = lax.dynamic_slice_in_dim(chosen, section * exits, exits, 0)
    own_square = jnp.take(squares, own_micro, axis=0).reshape(rows, 1)
    numbers = jnp.stack([section.astype(jnp.int32), jnp.int32(width)])
    latent, scale = run_chain(numbers, own_products, gram, own_square)

    head_gain = lax.dynamic_slice_in_dim(exit_norm_gain, section * head_rows, head_rows, 0)
    scaled_head = (head_weight.astype(f32) * head_gain[:, None]).astype(bf16)
    head = both_cores(scaled_head, 1)
    state_slice = lax.dynamic_slice_in_dim(inputs, section * head_rows, head_rows, 2)
    state_slice = jnp.take(state_slice, chosen, axis=0).reshape(sections, rows, head_rows)
    up_slice = lax.dynamic_slice_in_dim(up_rows, section * head_rows, head_rows, 2)
    left = jnp.concatenate([state_slice, up_slice], 1)
    left = spread(spread(left, "zlo"), "y")
    left = left.transpose(2, 1, 0, 3, 4)
    each = rows + own_rank
    partial = jnp.dot(
        left.reshape(sections * plane * each, head_rows), head, preferred_element_type=f32
    ).astype(bf16)
    partial = partial.reshape(2, 4, plane * each, 2 * head_columns)
    partial = lax.all_to_all(partial, "x", 1, 1, tiled=True)
    partial = jnp.sum(partial.astype(f32), 1).astype(bf16)
    partial = lax.all_to_all(partial, "zhi", 0, 0, tiled=True)
    total = jnp.sum(partial.astype(f32), 0).reshape(plane, each, 2 * head_columns)
    base = total[:, :rows].reshape(plane * rows, 2 * head_columns)
    correction = total[:, rows:].reshape(4, 4, own_rank, 2 * head_columns).astype(bf16)
    correction = correction.transpose(1, 0, 2, 3).reshape(-1, 2 * head_columns)
    correction = both_cores(spread(spread(correction, "zhi"), "x"), None)
    correction = correction.transpose(2, 1, 0, 3, 4).reshape(sections * rank, 2 * head_columns)

    high = lax.reduce_precision(scale, 8, 7)
    middle = lax.reduce_precision(scale - high, 8, 7)
    low = scale - high - middle
    parts = jnp.concatenate([high, middle, low], 1).astype(bf16)
    parts = jnp.pad(parts, ((0, 0), (0, 125)))
    latents = spread(jnp.concatenate([latent, parts], 1), PLANE)
    latents = latents.reshape(plane * rows, -1)
    scales = jnp.sum(latents[:, sections * rank :].astype(f32), 1, keepdims=True)
    logits = scales * (
        base + jnp.dot(latents[:, : sections * rank], correction, preferred_element_type=f32)
    )
    capped = LOGIT_CEILING * jnp.tanh(logits * RECIPROCAL_HEAT / LOGIT_CEILING)
    exp_total = jnp.sum(jnp.exp(capped), -1)
    wanted = jnp.take(targets, own_micro, axis=0).reshape(exits, plane, 2, tokens)
    wanted = lax.dynamic_index_in_dim(wanted, lax.axis_index("core"), 2, keepdims=False)
    wanted = wanted.transpose(1, 0, 2).reshape(plane * rows)
    start = lax.axis_index(PLANE) * (2 * head_columns)
    columns = jnp.arange(2 * head_columns, dtype=jnp.int32) + start
    picked = jnp.sum(jnp.where(columns[None, :] == wanted[:, None], capped, 0.0), -1)
    sums = jnp.stack([exp_total.reshape(plane, rows), picked.reshape(plane, rows)], 1)
    sums = jnp.sum(lax.all_to_all(sums, PLANE, 0, 0, tiled=True), 0)
    return (jnp.log(sums[0]) - sums[1]).reshape(1, exits, tokens)


def solution(mesh):
    devices = mesh.devices.reshape(2, 4, 4, 4, 2)
    split = Mesh(devices, SECTION + DP)
    placed = (
        P(None, DP, None),
        P(SECTION, None),
        P(SECTION, DP, None),
        P(SECTION, None, DP),
        P(),
        P(SECTION, DP),
        P(),
        P(),
    )
    return jax.shard_map(
        per_device, mesh=split, in_specs=placed, out_specs=P(SECTION, None, DP), check_vma=False
    )
```

```python
import jax
import jax.numpy as jnp
from jax import lax
from jax.experimental import pallas as pl
from jax.experimental.pallas import tpu as pltpu
from jax.sharding import Mesh, PartitionSpec as P

EPSILON = 1e-05
LOGIT_CEILING = 30.0
RECIPROCAL_HEAT = 1.0 / 0.7
INTERPRET = False

SECTION = ("zhi", "x")
DP = ("zlo", "y", "core")
PLANE = ("zlo", "y")
LINE = (0, 1, 2, 3)
RING = (0, 1, 3, 2)


def hop(block, axis, bit):
    size = lax.axis_size(axis)
    return lax.ppermute(block, axis, [(i, i ^ bit) for i in range(size)])


def ring(block, axis):
    half = block.shape[0] // 2
    one = hop(block, axis, 1)
    three = hop(block, axis, 3)
    return [block, one, three, hop(three[:half], axis, 1), hop(one[half:], axis, 3)]


def direct(block, axis, order):
    return [block] + [hop(block, axis, bit) for bit in order[1:]]


def spread(block, axis):
    size = lax.axis_size(axis)
    copies = jnp.broadcast_to(block[None], (size, *block.shape))
    return lax.all_to_all(copies, axis, 0, 0, tiled=True)


def chain_kernel(exit_ref, products_ref, gram_ref, square_ref, sent_ref, scale_ref, latent_ref):
    layers, _, twice = products_ref.shape
    rank = twice // 2
    width = exit_ref[1].astype(jnp.float32)
    square = square_ref[...]
    for layer in range(layers):
        here = slice(layer * rank, (layer + 1) * rank)
        before = slice(0, layer * rank)
        entering = products_ref[layer, :, :rank]
        cross = products_ref[layer, :, rank:]
        if layer > 0:
            earlier = latent_ref[:, before]
            entering += jnp.dot(earlier, gram_ref[before, here], preferred_element_type=jnp.float32)
            cross += lax.dot_general(
                earlier,
                gram_ref[here, before],
                (((1,), (1,)), ((), ())),
                preferred_element_type=jnp.float32,
            )
        value = entering * lax.rsqrt(square / width + EPSILON)
        latent = (value / (1.0 + jnp.exp(-value))).astype(jnp.bfloat16)
        latent = jnp.where(layer <= exit_ref[0], latent, jnp.zeros_like(latent))
        latent_ref[:, here] = latent
        apart = (exit_ref[0] % 4) ^ (layer % 4)
        spot = (apart ^ (apart >> 1)) * 2 + layer // 4
        sent_ref[:, pl.ds(pl.multiple_of(spot * rank, rank), rank)] = latent
        own = jnp.dot(latent, gram_ref[here, here], preferred_element_type=jnp.float32)
        grown = latent.astype(jnp.float32) * (2.0 * cross + own)
        square = jnp.maximum(square + jnp.sum(grown, -1, keepdims=True), 0.0)
    scale_ref[...] = lax.rsqrt(square / width + EPSILON)


def run_chain(numbers, products, gram, square):
    layers, rows, twice = products.shape
    whole = pl.BlockSpec(memory_space=pltpu.VMEM)
    return pl.pallas_call(
        chain_kernel,
        out_shape=(
            jax.ShapeDtypeStruct((rows, layers * twice // 2), jnp.bfloat16),
            jax.ShapeDtypeStruct((rows, 1), jnp.float32),
        ),
        in_specs=[pl.BlockSpec(memory_space=pltpu.SMEM), whole, whole, whole],
        out_specs=(whole, whole),
        scratch_shapes=[pltpu.VMEM((rows, layers * twice // 2), jnp.bfloat16)],
        compiler_params=pltpu.CompilerParams(vmem_limit_bytes=16 * 2**20),
        interpret=INTERPRET,
    )(numbers, products, gram, square)


def per_device(
    inputs, layer_gain, layer_down, layer_up, exit_norm_gain, head_weight, targets, exit_section
):
    f32, bf16 = jnp.float32, jnp.bfloat16
    section = lax.axis_index(SECTION)
    place = lax.axis_index(DP)
    micro, tokens, width = inputs.shape
    sections = lax.axis_size(SECTION)
    plane = lax.axis_size(PLANE)
    rank = layer_up.shape[1]
    own_rank = rank // lax.axis_size(DP)
    exits = micro // sections
    rows = exits * tokens
    head_rows, head_columns = head_weight.shape

    order = jnp.arange(micro, dtype=jnp.int32)
    same = exit_section[:, None] == exit_section[None, :]
    ranks = jnp.sum((same & (order[:, None] > order[None, :])).astype(jnp.int32), 1)
    slot = exit_section * exits + ranks
    chosen = jnp.sum(jnp.where(slot[None, :] == order[:, None], order[None, :], 0), 1)

    zhi, x, zlo, y, core = (lax.axis_index(name) for name in SECTION + DP)
    lines, rings = jnp.array(LINE, jnp.int32), jnp.array(RING, jnp.int32)
    near_z, near_y, near_x = zlo ^ lines, y ^ rings, x ^ rings
    first = core == 0

    down = layer_down[0]
    up = layer_up[0]
    features = down.shape[0]
    gain = lax.dynamic_slice_in_dim(layer_gain[0], place * features, features, 0)
    scaled_down = (down.astype(f32) * gain[:, None]).astype(bf16)
    pair = jnp.concatenate([scaled_down, up.T], 1)
    maps = ring(jnp.concatenate(direct(pair, "zlo", LINE), 0), "y")
    maps = maps + [hop(piece, "core", 1) for piece in maps]
    near_core = jnp.stack([core, 1 - core])
    blocks = (near_z[None, None, :] * 4 + near_y[None, :, None]) * 2 + near_core[:, None, None]
    blocks = blocks.reshape(-1)

    sent = up.reshape(2, 4, 4, own_rank, features).transpose(2, 1, 0, 3, 4)
    sent = sent.reshape(-1, own_rank, features)
    came = lax.all_to_all(sent, DP, 0, 0, tiled=True)
    up_own = came.transpose(1, 0, 2).reshape(own_rank, width)
    up_rows = spread(up_own, SECTION)

    wide = inputs.astype(f32)
    squares = jnp.sum(wide * wide, -1)
    flat = inputs.reshape(micro * tokens, width // features, features)
    flat = jnp.take(flat, blocks, axis=1).reshape(micro * tokens, width)
    up_flat = up_rows.reshape(sections * own_rank, width // features, features)
    up_flat = jnp.take(up_flat, blocks, axis=1).reshape(sections * own_rank, width)
    flat = jnp.concatenate([flat, up_flat], 0)
    products, start = 0.0, 0
    for piece in maps:
        stop = start + piece.shape[0]
        products += jnp.dot(flat[:, start:stop], piece, preferred_element_type=f32)
        start = stop
    state_part = jnp.take(products[: micro * tokens].reshape(micro, tokens, -1), chosen, axis=0)
    state_part = state_part.reshape(sections, rows, 2, rank).transpose(0, 2, 1, 3)
    gram_part = products[micro * tokens :].reshape(sections, own_rank, 2 * rank)
    ahead = (jnp.arange(sections, dtype=jnp.int32) < section)[:, None, None]
    gram_part = jnp.where(ahead, gram_part[..., :rank], gram_part[..., rank:])
    gram_part = gram_part.reshape(sections * own_rank, rank)
    outgoing = jnp.concatenate(
        [
            state_part.reshape(sections, 2 * rows, rank),
            jnp.broadcast_to(gram_part[None], (sections, *gram_part.shape)),
        ],
        1,
    )
    incoming = lax.all_to_all(outgoing, SECTION, 0, 0, tiled=True)
    own_products = incoming[:, : 2 * rows].reshape(sections, 2, rows, rank)
    own_products = own_products.transpose(0, 2, 1, 3).reshape(sections, rows, 2 * rank)

    gram = incoming[:, 2 * rows :].transpose(1, 0, 2).astype(bf16)
    gram = gram.reshape(sections * own_rank, sections * rank)
    gram = direct(jnp.concatenate(direct(gram, "zlo", LINE), 0), "y", RING)
    gram = gram + [hop(piece, "core", 1) for piece in gram]
    at = (near_core[:, None, None] * 4 + near_y[None, :, None]) * 4 + near_z[None, None, :]
    at = at.reshape(-1, 1, 1) * own_rank + jnp.arange(own_rank, dtype=jnp.int32)
    at = at + jnp.arange(sections, dtype=jnp.int32)[:, None] * rank
    sorting = (jnp.arange(sections * rank, dtype=jnp.int32)[:, None] == at.reshape(1, -1)).astype(
        bf16
    )
    gram = jnp.dot(sorting, jnp.concatenate(gram, 0), preferred_element_type=f32).astype(bf16)

    own_micro = lax.dynamic_slice_in_dim(chosen, section * exits, exits, 0)
    own_square = jnp.take(squares, own_micro, axis=0).reshape(rows, 1)
    numbers = jnp.stack([section.astype(jnp.int32), jnp.int32(width)])
    latent, scale = run_chain(numbers, own_products, gram, own_square)

    head_gain = lax.dynamic_slice_in_dim(exit_norm_gain, section * head_rows, head_rows, 0)
    scaled_head = (head_weight.astype(f32) * head_gain[:, None]).astype(bf16)
    head = jnp.concatenate(ring(scaled_head, "x"), 0)
    head = jnp.concatenate([head, hop(head, "core", 1)], 1)

    def half_of(array, which):
        part = lax.dynamic_slice_in_dim(array, which * 4 * head_rows, 4 * head_rows, array.ndim - 1)
        part = part.reshape(-1, 4, head_rows)
        return jnp.take(part, near_x, axis=1).reshape(-1, 4 * head_rows)

    def state_block(which):
        mine = lax.dynamic_slice_in_dim(chosen, (which * 4 + x) * exits, exits, 0)
        return half_of(jnp.take(inputs, mine, axis=0), zhi)

    def partial_logits(block):
        left = ring(jnp.concatenate(direct(block, "zlo", LINE), 0), "y")
        return jnp.dot(jnp.concatenate(left, 0), head, preferred_element_type=f32)

    passed = partial_logits(state_block(1 - zhi)).astype(bf16)
    base = partial_logits(state_block(zhi)) + hop(passed, "zhi", 1).astype(f32)

    other_up = hop(half_of(up_own, 1 - zhi), "zhi", 1)
    own_up = half_of(up_own, zhi)
    up_block = jnp.where(
        zhi == 0, jnp.concatenate([own_up, other_up]), jnp.concatenate([other_up, own_up])
    )
    left = direct(jnp.concatenate(direct(up_block, "zlo", LINE), 0), "y", RING)
    correction = jnp.dot(jnp.concatenate(left, 0), head, preferred_element_type=f32)
    correction = correction + hop(correction.astype(bf16), "zhi", 1).astype(f32)
    correction = correction.astype(bf16).reshape(plane, 2 * own_rank, 2 * head_columns)
    steps = jnp.arange(4, dtype=jnp.int32)
    apart = y ^ steps
    back = ((apart ^ (apart >> 1)) * 4)[:, None] + (zlo ^ steps)[None, :]
    correction = jnp.take(correction, back.reshape(-1), axis=0)
    correction = correction.reshape(plane, 2, own_rank, 2 * head_columns).transpose(1, 0, 2, 3)
    correction = correction.reshape(rank, 2 * head_columns)
    correction = jnp.concatenate(direct(correction, "x", RING), 0)
    turned = jnp.concatenate([correction[:, head_columns:], correction[:, :head_columns]], 1)
    turned = hop(turned, "core", 1).reshape(sections, rank // 2, 2 * head_columns)
    correction = correction.reshape(sections, rank // 2, 2 * head_columns)
    correction = jnp.stack(
        [jnp.where(first, correction, turned), jnp.where(first, turned, correction)], 1
    )
    correction = correction.reshape(sections * rank, 2 * head_columns)

    high = lax.reduce_precision(scale, 8, 7)
    middle = lax.reduce_precision(scale - high, 8, 7)
    low = scale - high - middle
    parts = jnp.concatenate([high, middle, low], 1).astype(bf16)
    parts = jnp.pad(parts, ((0, 0), (0, 125)))
    latents = jnp.concatenate(direct(jnp.concatenate([latent, parts], 1), "zlo", LINE), 0)
    latents = jnp.concatenate(direct(latents, "y", RING), 0)
    scales = jnp.sum(latents[:, sections * rank :].astype(f32), 1, keepdims=True)
    logits = scales * (
        base + jnp.dot(latents[:, : sections * rank], correction, preferred_element_type=f32)
    )
    capped = LOGIT_CEILING * jnp.tanh(logits * RECIPROCAL_HEAT / LOGIT_CEILING)
    exp_total = jnp.sum(jnp.exp(capped), -1)
    wanted = jnp.take(targets, own_micro, axis=0).reshape(exits, 4, 4, 2, tokens)
    wanted = lax.dynamic_index_in_dim(wanted, core, 3, keepdims=False)
    wanted = jnp.take(jnp.take(wanted, near_z, axis=1), near_y, axis=2)
    wanted = wanted.transpose(2, 1, 0, 3).reshape(plane * rows)
    begin = (zlo * 4 + y) * 2 + near_core
    columns = begin[:, None] * head_columns + jnp.arange(head_columns, dtype=jnp.int32)
    columns = columns.reshape(-1)
    picked = jnp.sum(jnp.where(columns[None, :] == wanted[:, None], capped, 0.0), -1)
    sums = jnp.stack([exp_total.reshape(4, 4, rows), picked.reshape(4, 4, rows)], 2)
    sums = sums[0] + sum(hop(sums[i], "y", RING[i]) for i in (1, 2, 3))
    sums = sums[0] + sum(hop(sums[i], "zlo", LINE[i]) for i in (1, 2, 3))
    return (jnp.log(sums[0]) - sums[1]).reshape(1, exits, tokens)


def solution(mesh):
    devices = mesh.devices.reshape(2, 4, 4, 4, 2)
    split = Mesh(devices, SECTION + DP)
    placed = (
        P(None, DP, None),
        P(SECTION, None),
        P(SECTION, DP, None),
        P(SECTION, None, DP),
        P(),
        P(SECTION, DP),
        P(),
        P(),
    )
    return jax.shard_map(
        per_device, mesh=split, in_specs=placed, out_specs=P(SECTION, None, DP), check_vma=False
    )
```

```python
import functools

import jax
import jax.numpy as jnp
from jax import lax
from jax.experimental import pallas as pl
from jax.experimental.pallas import tpu as pltpu
from jax.sharding import Mesh, PartitionSpec as P

EPSILON = 1e-05
LOGIT_CEILING = 30.0
RECIPROCAL_HEAT = 1.0 / 0.7
INTERPRET = False

SECTION = ("zhi", "x")
DP = ("zlo", "y", "core")
PLANE = ("zlo", "y")
LINE = (0, 1, 2, 3)
RING = (0, 1, 3, 2)
F32, BF16 = jnp.float32, jnp.bfloat16


def hop(block, axis, bit):
    size = lax.axis_size(axis)
    return lax.ppermute(block, axis, [(i, i ^ bit) for i in range(size)])


def ring(block, axis):
    half = block.shape[0] // 2
    one = hop(block, axis, 1)
    three = hop(block, axis, 3)
    return [block, one, three, hop(three[:half], axis, 1), hop(one[half:], axis, 3)]


def direct(block, axis, order):
    return [block] + [hop(block, axis, bit) for bit in order[1:]]


def kernel_call(body, out, scalars, arrays, after=(), scratch=(), limit=48):
    whole = pl.BlockSpec(memory_space=pltpu.VMEM)
    small = pl.BlockSpec(memory_space=pltpu.SMEM)
    unread = pl.BlockSpec(memory_space=pl.ANY)
    count = len(scalars) + len(arrays)

    def inner(*refs):
        body(*refs[:count], *refs[count + len(after) :])

    shapes = [jax.ShapeDtypeStruct(shape, dtype) for shape, dtype, _ in out]
    return pl.pallas_call(
        inner,
        out_shape=shapes,
        in_specs=[small] * len(scalars) + [whole] * len(arrays) + [unread] * len(after),
        out_specs=[whole if space == "v" else small for _, _, space in out],
        scratch_shapes=list(scratch),
        compiler_params=pltpu.CompilerParams(vmem_limit_bytes=limit * 2**20),
        interpret=INTERPRET,
    )(*scalars, *arrays, *after)


def gray(value):
    return value ^ (value >> 1)


def nearby(where_ref, index):
    return (where_ref[2] ^ (index % 4)) * 4 + (where_ref[3] ^ gray(index // 4))


def rows_kernel(where_ref, exits_ref, inputs_ref, own_ref, other_ref, square_ref, rows_ref, chosen_ref, count_ref):
    micro, tokens, width = inputs_ref.shape
    sections = 8
    exits = micro // sections
    each = exits * tokens
    for section in range(sections):
        count_ref[section] = 0
    for index in range(micro):
        section = exits_ref[index]
        spot = count_ref[section]
        count_ref[section] = spot + 1
        chosen_ref[section * exits + spot] = index
    for section in range(sections):
        parts = [
            inputs_ref[chosen_ref[section * exits + spot]].astype(F32) for spot in range(exits)
        ]
        rows_ref[section * each : (section + 1) * each, :] = jnp.concatenate(parts, 0).astype(BF16)
    own = rows_ref[pl.ds(pl.multiple_of(where_ref[5] * each, each), each), :].astype(F32)
    square_ref[...] = jnp.sum(own * own, -1, keepdims=True)
    block = width // 32
    for index in range(16):
        start = nearby(where_ref, index) * 2 * block
        here = slice(index * block, (index + 1) * block)
        mine = pl.multiple_of(start + where_ref[4] * block, block)
        theirs = pl.multiple_of(start + (1 - where_ref[4]) * block, block)
        own_ref[:, here] = rows_ref[:, pl.ds(mine, block)]
        other_ref[:, here] = rows_ref[:, pl.ds(theirs, block)]


def state_kernel(where_ref, rows_ref, out_ref):
    each = out_ref.shape[0] // 2
    quarter = out_ref.shape[1] // 4
    zhi, x = where_ref[0], where_ref[1]
    for spot, half in ((0, 1 - zhi), (1, zhi)):
        begin = pl.multiple_of((half * 4 + x) * each, each)
        for index in range(4):
            start = pl.multiple_of((zhi * 4 + (x ^ gray(index))) * quarter, quarter)
            out_ref[spot * each : (spot + 1) * each, index * quarter : (index + 1) * quarter] = (
                rows_ref[pl.ds(begin, each), pl.ds(start, quarter)]
            )


def up_kernel(where_ref, came_ref, out_ref):
    block = came_ref.shape[2]
    for index in range(came_ref.shape[0]):
        piece = came_ref[nearby(where_ref, index)]
        for copy in range(out_ref.shape[0]):
            out_ref[copy, :, index * block : (index + 1) * block] = piece


def halves_kernel(where_ref, first_ref, second_ref, own_ref, other_ref):
    block = first_ref.shape[2]
    zhi, x = where_ref[0], where_ref[1]
    for ref, half in ((own_ref, zhi), (other_ref, 1 - zhi)):
        for index in range(4):
            at = x ^ gray(index)
            z = half * 2 + (at >> 1)
            for low in range(2):
                y = (at & 1) * 2 + low
                for core, came_ref in enumerate((first_ref, second_ref)):
                    start = (index * 4 + low * 2 + core) * block
                    ref[:, start : start + block] = came_ref[z * 4 + y]


def products_kernel(where_ref, own_ref, other_ref, up_ref, *refs):
    pieces, (keep_ref, send_ref) = refs[:-2], refs[-2:]
    rows = own_ref.shape[0]
    rank = keep_ref.shape[1]
    section, core = where_ref[5], where_ref[4]
    total, start = 0.0, 0
    for piece in pieces:
        here = slice(start, start + piece.shape[0])
        left = jnp.concatenate([own_ref[:, here], other_ref[:, here], up_ref[:, here]], 0)
        total += jnp.dot(left, piece[...], preferred_element_type=F32)
        start += piece.shape[0]
    each = rows // 8
    for ref, begin in ((keep_ref, 0), (send_ref, rows)):
        for index in range(8):
            part = total[begin + index * each : begin + (index + 1) * each]
            ref[index * 2 * each : (index * 2 + 1) * each] = part[:, :rank]
            ref[(index * 2 + 1) * each : (index * 2 + 2) * each] = part[:, rank:]
    up_rows = up_ref.shape[0] // 8
    layers = []
    for layer in range(8):
        part = total[2 * rows + layer * up_rows : 2 * rows + (layer + 1) * up_rows]
        layers.append(jnp.where(layer < section, part[:, :rank], part[:, rank:]))
    low = jnp.concatenate(layers[:4], 0)
    high = jnp.concatenate(layers[4:], 0)
    keep_ref[2 * rows :] = jnp.where(core == 0, low, high)
    send_ref[2 * rows :] = jnp.where(core == 0, high, low)


def combine_kernel(keep_ref, came_ref, out_ref):
    sections, each, _ = out_ref.shape
    half = each // 2
    shared = keep_ref[sections * half :] + came_ref[sections * half :]
    for index in range(sections):
        here = slice(index * half, (index + 1) * half)
        out_ref[index, :half] = keep_ref[here] + came_ref[here]
        out_ref[index, half:] = shared


def gram_kernel(incoming_ref, out_ref):
    sections, each, rank = incoming_ref.shape
    for index in range(sections):
        out_ref[:, index * rank : (index + 1) * rank] = incoming_ref[index, each // 2 :].astype(
            BF16
        )


def chain_kernel(where_ref, products_ref, gram_ref, square_ref, sent_ref, latent_ref):
    layers, each, rank = products_ref.shape
    rows = each // 4
    width = where_ref[6].astype(F32)
    square = square_ref[...]
    for layer in range(layers):
        here = slice(layer * rank, (layer + 1) * rank)
        before = slice(0, layer * rank)
        entering = products_ref[layer, :rows]
        cross = products_ref[layer, rows : 2 * rows]
        if layer > 0:
            earlier = latent_ref[:, before]
            entering += jnp.dot(earlier, gram_ref[before, here], preferred_element_type=F32)
            cross += lax.dot_general(
                earlier,
                gram_ref[here, before],
                (((1,), (1,)), ((), ())),
                preferred_element_type=F32,
            )
        value = entering * lax.rsqrt(square / width + EPSILON)
        latent = (value / (1.0 + jnp.exp(-value))).astype(BF16)
        latent = jnp.where(layer <= where_ref[5], latent, jnp.zeros_like(latent))
        latent_ref[:, here] = latent
        spot = gray(where_ref[1] ^ (layer % 4)) * 2 + layer // 4
        sent_ref[:, pl.ds(pl.multiple_of(spot * rank, rank), rank)] = latent
        own = jnp.dot(latent, gram_ref[here, here], preferred_element_type=F32)
        grown = latent.astype(F32) * (2.0 * cross + own)
        square = jnp.maximum(square + jnp.sum(grown, -1, keepdims=True), 0.0)
    scale = lax.rsqrt(square / width + EPSILON)
    scale = jnp.broadcast_to(scale, (rows, rank))
    lane = lax.broadcasted_iota(jnp.int32, (rows, rank), 1)
    high = scale.astype(BF16).astype(F32)
    middle = (scale - high).astype(BF16).astype(F32)
    low = scale - high - middle
    parts = jnp.where(lane == 0, high, jnp.where(lane == 1, middle, low))
    parts = jnp.where(lane < 3, parts, 0.0)
    sent_ref[:, layers * rank :] = parts.astype(BF16)


def per_device(
    inputs, layer_gain, layer_down, layer_up, exit_norm_gain, head_weight, targets, exit_section
):
    section = lax.axis_index(SECTION)
    place = lax.axis_index(DP)
    zhi, x, zlo, y, core = (lax.axis_index(name) for name in SECTION + DP)
    micro, tokens, width = inputs.shape
    sections = lax.axis_size(SECTION)
    plane = lax.axis_size(PLANE)
    rank = layer_up.shape[1]
    own_rank = rank // plane
    exits = micro // sections
    rows = exits * tokens
    head_rows, head_columns = head_weight.shape
    near_z, near_y = zlo ^ jnp.array(LINE, jnp.int32), y ^ jnp.array(RING, jnp.int32)
    where = jnp.stack([zhi, x, zlo, y, core, section, jnp.int32(width)]).astype(jnp.int32)

    up = layer_up[0]
    features = up.shape[1]
    gain = lax.dynamic_slice_in_dim(layer_gain[0], place * features, features, 0)
    scaled_down = (layer_down[0].astype(F32) * gain[:, None]).astype(BF16)
    pair = jnp.concatenate([scaled_down, up.T], 1)
    lined = jnp.concatenate(direct(pair, "zlo", LINE), 0)
    maps = ring(lined, "y")

    came = lax.all_to_all(up, PLANE, 0, 0, tiled=True).reshape(plane, own_rank, features)
    (copies,) = kernel_call(
        up_kernel, [((sections, own_rank, width // 2), BF16, "v")], [where], [came]
    )
    up_rows = lax.all_to_all(copies, SECTION, 0, 0, tiled=True)
    up_rows = up_rows.reshape(sections * own_rank, width // 2)

    own_rows, other_rows, own_square, all_rows, chosen = kernel_call(
        rows_kernel,
        [
            ((sections * rows, width // 2), BF16, "v"),
            ((sections * rows, width // 2), BF16, "v"),
            ((rows, 1), F32, "v"),
            ((sections * rows, width), BF16, "v"),
            ((micro,), jnp.int32, "s"),
        ],
        [where, exit_section],
        [inputs],
        scratch=[pltpu.SMEM((sections,), jnp.int32)],
    )
    partner_rows = hop(other_rows, "core", 1)

    sums = ((2 * sections * rows + 4 * own_rank, rank), F32, "v")
    keep, send = kernel_call(
        products_kernel, [sums, sums], [where], [own_rows, partner_rows, up_rows, *maps]
    )
    (outgoing,) = kernel_call(
        combine_kernel, [((sections, 4 * rows, rank), F32, "v")], [], [keep, hop(send, "core", 1)]
    )
    incoming = lax.all_to_all(outgoing, SECTION, 0, 0, tiled=True)

    (gram,) = kernel_call(
        gram_kernel, [((4 * own_rank, sections * rank), BF16, "v")], [], [incoming]
    )
    gram = jnp.concatenate(direct(gram, "zlo", LINE), 0)
    gram = jnp.concatenate(direct(gram, "y", RING), 0)
    steps = jnp.arange(4, dtype=jnp.int32)
    at = ((near_z[None, :] * 4 + near_y[:, None]) * own_rank)[..., None, None]
    at = at + (steps * rank)[:, None] + jnp.arange(own_rank, dtype=jnp.int32)
    at = at.reshape(-1)
    line = jnp.arange(sections * rank, dtype=jnp.int32)[:, None]
    own_sorting = (line == (at + core * 4 * rank)[None, :]).astype(BF16)
    other_sorting = (line == (at + (1 - core) * 4 * rank)[None, :]).astype(BF16)
    gram = jnp.dot(own_sorting, gram, preferred_element_type=F32) + jnp.dot(
        other_sorting, hop(gram, "core", 1), preferred_element_type=F32
    )
    (latents,) = kernel_call(
        chain_kernel,
        [((rows, (sections + 1) * rank), BF16, "v")],
        [where],
        [incoming, gram.astype(BF16), own_square],
        scratch=[pltpu.VMEM((rows, sections * rank), BF16)],
    )

    head_gain = lax.dynamic_slice_in_dim(exit_norm_gain, section * head_rows, head_rows, 0)
    scaled_head = (head_weight.astype(F32) * head_gain[:, None]).astype(BF16)
    head = jnp.concatenate(ring(scaled_head, "x"), 0)
    other_head = hop(head, "core", 1)

    def through(left):
        return jnp.concatenate(
            [
                jnp.dot(left, head, preferred_element_type=F32),
                jnp.dot(left, other_head, preferred_element_type=F32),
            ],
            1,
        )

    partner_came = hop(came, "core", 1)
    first = core == 0
    own_half, other_half = kernel_call(
        halves_kernel,
        [((own_rank, width // 2), BF16, "v")] * 2,
        [where],
        [jnp.where(first, came, partner_came), jnp.where(first, partner_came, came)],
        after=[lined],
    )
    up_block = jnp.where(core == zhi, own_half, hop(other_half, "zhi", 1))
    left = direct(jnp.concatenate(direct(up_block, "zlo", LINE), 0), "y", RING)
    correction = through(jnp.concatenate(left, 0))
    correction = correction + hop(correction.astype(BF16), "zhi", 1).astype(F32)
    correction = correction.astype(BF16).reshape(plane, own_rank, 2 * head_columns)
    back = gray(y ^ steps)[None, :] * 4 + (zlo ^ steps)[:, None]
    correction = jnp.take(correction, back.reshape(-1), axis=0)
    correction = correction.reshape(rank, 2 * head_columns)
    correction = jnp.concatenate(direct(correction, "x", RING), 0)
    turned = jnp.concatenate([correction[:, head_columns:], correction[:, :head_columns]], 1)
    turned = hop(turned, "core", 1).reshape(4, 1, rank, 2 * head_columns)
    correction = correction.reshape(4, 1, rank, 2 * head_columns)
    correction = jnp.concatenate(
        [jnp.where(first, correction, turned), jnp.where(first, turned, correction)], 1
    )
    correction = correction.reshape(sections * rank, 2 * head_columns)

    (state,) = kernel_call(
        state_kernel,
        [((2 * rows, width // 2), BF16, "v")],
        [where],
        [all_rows],
        after=[lined],
    )
    state = jnp.concatenate(direct(state, "zlo", LINE), 0).reshape(4, 2 * rows, width // 2)
    state = ring(state, "y")
    near = through(jnp.concatenate(state[:3], 0).reshape(-1, width // 2))
    near = near.reshape(12, 2, rows, 2 * head_columns)
    far = through(jnp.concatenate(state[3:], 0).reshape(-1, width // 2))
    far = far.reshape(4, 2, rows, 2 * head_columns)
    near = near[:, 1] + hop(near[:, 0].astype(BF16), "zhi", 1).astype(F32)
    far = far[:, 1] + hop(far[:, 0].astype(BF16), "zhi", 1).astype(F32)
    base = jnp.concatenate([near, far], 0).reshape(plane * rows, 2 * head_columns)

    latents = jnp.concatenate(direct(latents, "zlo", LINE), 0)
    latents = jnp.concatenate(direct(latents, "y", RING), 0)
    scales = jnp.sum(latents[:, sections * rank :].astype(F32), 1, keepdims=True)
    logits = scales * (
        base + jnp.dot(latents[:, : sections * rank], correction, preferred_element_type=F32)
    )
    capped = LOGIT_CEILING * jnp.tanh(logits * RECIPROCAL_HEAT / LOGIT_CEILING)
    exp_total = jnp.sum(jnp.exp(capped), -1)
    own_micro = lax.dynamic_slice_in_dim(chosen, section * exits, exits, 0)
    wanted = jnp.take(targets, own_micro, axis=0).reshape(exits, 4, 4, 2, tokens)
    wanted = lax.dynamic_index_in_dim(wanted, core, 3, keepdims=False)
    wanted = jnp.take(jnp.take(wanted, near_z, axis=1), near_y, axis=2)
    wanted = wanted.transpose(2, 1, 0, 3).reshape(plane * rows)
    begin = (zlo * 4 + y) * 2 + jnp.stack([core, 1 - core])
    columns = begin[:, None] * head_columns + jnp.arange(head_columns, dtype=jnp.int32)
    columns = columns.reshape(-1)
    picked = jnp.sum(jnp.where(columns[None, :] == wanted[:, None], capped, 0.0), -1)
    sums = jnp.stack([exp_total.reshape(4, 4, rows), picked.reshape(4, 4, rows)], 2)
    sums = sums[0] + sum(hop(sums[i], "y", RING[i]) for i in (1, 2, 3))
    sums = sums[0] + sum(hop(sums[i], "zlo", LINE[i]) for i in (1, 2, 3))
    return (jnp.log(sums[0]) - sums[1]).reshape(1, exits, tokens)


def solution(mesh):
    split = Mesh(mesh.devices.reshape(2, 4, 4, 4, 2), SECTION + DP)
    placed = (
        P(None, DP, None),
        P(SECTION, None),
        P(SECTION, DP, None),
        P(SECTION, None, DP),
        P(),
        P(SECTION, DP),
        P(),
        P(),
    )
    return jax.shard_map(
        per_device, mesh=split, in_specs=placed, out_specs=P(SECTION, None, DP), check_vma=False
    )
```

```python
import math

import functools

import jax
import jax.numpy as jnp
from jax import lax
from jax.experimental import pallas as pl
from jax.experimental.pallas import tpu as pltpu
from jax.sharding import Mesh, PartitionSpec as P

EPSILON = 1e-05
LOGIT_CEILING = 30.0
RECIPROCAL_HEAT = 1.0 / 0.7
INTERPRET = False

SECTION = ("zhi", "x")
DP = ("zlo", "y", "core")
PLANE = ("zlo", "y")
LINE = (0, 1, 2, 3)
RING = (0, 1, 3, 2)
F32, BF16 = jnp.float32, jnp.bfloat16


def hop(block, axis, bit):
    size = lax.axis_size(axis)
    return lax.ppermute(block, axis, [(i, i ^ bit) for i in range(size)])


def ring(low, high, axis):
    three_low = hop(low, axis, 3)
    one_high = hop(high, axis, 1)
    one_low = hop(low, axis, 1)
    three_high = hop(high, axis, 3)
    far_low = hop(three_low, axis, 1)
    far_high = hop(one_high, axis, 3)
    return [low, one_low, three_low, far_low], [high, one_high, three_high, far_high]


def tied(value, *others):
    return lax.optimization_barrier((value, *others))[0]


def spread(block, axis):
    size = lax.axis_size(axis)
    copies = jnp.broadcast_to(block[None], (size, *block.shape))
    return lax.all_to_all(copies, axis, 0, 0, tiled=True)


def direct(block, axis, order):
    return [block] + [hop(block, axis, bit) for bit in order[1:]]


def kernel_call(body, out, scalars, arrays, after=(), scratch=()):
    whole = pl.BlockSpec(memory_space=pltpu.VMEM)
    small = pl.BlockSpec(memory_space=pltpu.SMEM)
    unread = pl.BlockSpec(memory_space=pl.ANY)
    count = len(scalars) + len(arrays)

    def inner(*refs):
        body(*refs[:count], *refs[count + len(after) :])

    shapes = [jax.ShapeDtypeStruct(shape, dtype) for shape, dtype, _ in out]
    sizes = [math.prod(one.shape) * one.dtype.itemsize for one in [*shapes, *arrays]]
    limit = 6 + 5 * sum(sizes) // 2**22
    return pl.pallas_call(
        inner,
        out_shape=shapes,
        in_specs=[small] * len(scalars) + [whole] * len(arrays) + [unread] * len(after),
        out_specs=[whole if space == "v" else small for _, _, space in out],
        scratch_shapes=list(scratch),
        compiler_params=pltpu.CompilerParams(vmem_limit_bytes=limit * 2**20),
        interpret=INTERPRET,
    )(*scalars, *arrays, *after)


def gray(value):
    return value ^ (value >> 1)


def stack_kernel(*refs):
    out_ref = refs[-1]
    start = 0
    for ref in refs[:-1]:
        out_ref[start : start + ref.shape[0]] = ref[...]
        start += ref.shape[0]


def stack(pieces):
    total = sum(piece.shape[0] for piece in pieces)
    shape = (total, *pieces[0].shape[1:])
    return kernel_call(stack_kernel, [(shape, pieces[0].dtype, "v")], [], pieces)[0]


def block_at(where_ref, index):
    return (where_ref[2] ^ (index % 4)) * 4 + (where_ref[3] ^ gray(index // 4))


def rows_kernel(
    where_ref,
    exits_ref,
    inputs_ref,
    targets_ref,
    own_ref,
    other_ref,
    square_ref,
    rows_ref,
    wanted_ref,
    chosen_ref,
    count_ref,
):
    micro, tokens, width = inputs_ref.shape
    sections = 8
    exits = micro // sections
    each = exits * tokens
    zlo, y, core, section = where_ref[2], where_ref[3], where_ref[4], where_ref[5]
    for index in range(sections):
        count_ref[index] = 0
    for index in range(micro):
        place = exits_ref[index]
        spot = count_ref[place]
        count_ref[place] = spot + 1
        chosen_ref[place * exits + spot] = index
    for place in range(sections):
        parts = [inputs_ref[chosen_ref[place * exits + spot]].astype(F32) for spot in range(exits)]
        rows_ref[place * each : (place + 1) * each, :] = jnp.concatenate(parts, 0).astype(BF16)
    own = rows_ref[pl.ds(pl.multiple_of(section * each, each), each), :].astype(F32)
    square_ref[...] = jnp.sum(own * own, -1, keepdims=True)
    block = width // 32
    for index in range(16):
        start = block_at(where_ref, index) * 2 * block
        here = slice(index * block, (index + 1) * block)
        mine = pl.multiple_of(start + core * block, block)
        theirs = pl.multiple_of(start + (1 - core) * block, block)
        own_ref[:, here] = rows_ref[:, pl.ds(mine, block)]
        other_ref[:, here] = rows_ref[:, pl.ds(theirs, block)]
    lanes = targets_ref.shape[1]
    ids = [
        jnp.broadcast_to(targets_ref[pl.ds(chosen_ref[section * exits + spot], 1), :], (tokens, lanes))
        for spot in range(exits)
    ]
    ids = jnp.concatenate(ids * 16, 0)
    row = lax.broadcasted_iota(jnp.int32, ids.shape, 0)
    lane = lax.broadcasted_iota(jnp.int32, ids.shape, 1)
    ring_step = row // (4 * each)
    from_y = y ^ gray(ring_step)
    from_z = zlo ^ (row // each % 4)
    token = ((from_z * 4 + from_y) * 2 + core) * tokens + row % tokens
    wanted_ref[...] = jnp.sum(jnp.where(lane == token, ids, 0), -1, keepdims=True)


def state_kernel(where_ref, rows_ref, out_ref):
    each = out_ref.shape[0] // 2
    quarter = out_ref.shape[1] // 4
    zhi, x = where_ref[0], where_ref[1]
    for spot, half in ((0, 1 - zhi), (1, zhi)):
        begin = pl.multiple_of((half * 4 + x) * each, each)
        for index in range(4):
            start = pl.multiple_of((zhi * 4 + (x ^ gray(index))) * quarter, quarter)
            out_ref[spot * each : (spot + 1) * each, index * quarter : (index + 1) * quarter] = (
                rows_ref[pl.ds(begin, each), pl.ds(start, quarter)]
            )


def pair_kernel(first_ref, second_ref, out_ref):
    each = first_ref.shape[0] // 2
    out_ref[:each] = first_ref[:each]
    out_ref[each : 2 * each] = second_ref[:each]
    out_ref[2 * each : 3 * each] = first_ref[each:]
    out_ref[3 * each :] = second_ref[each:]


def part_kernel(first_ref, second_ref, low_ref, high_ref):
    each = first_ref.shape[0] // 2
    low_ref[:each] = first_ref[:each]
    low_ref[each:] = second_ref[:each]
    high_ref[:each] = first_ref[each:]
    high_ref[each:] = second_ref[each:]


def up_kernel(where_ref, came_ref, out_ref):
    block = came_ref.shape[2]
    for index in range(came_ref.shape[0]):
        piece = came_ref[block_at(where_ref, index)]
        for copy in range(out_ref.shape[0]):
            out_ref[copy, :, index * block : (index + 1) * block] = piece


def leaving_kernel(where_ref, lined_ref, out_ref):
    for z in range(2):
        at = ((1 - where_ref[0]) * 2 + z) ^ where_ref[2]
        out_ref[z] = lined_ref[at, :, out_ref.shape[2] :]


def products_kernel(where_ref, own_ref, other_ref, up_ref, *refs):
    pieces, (keep_ref, send_ref, stay_ref) = refs[:-3], refs[-3:]
    rows = own_ref.shape[0]
    rank = keep_ref.shape[1]
    zhi, zlo, core, section = where_ref[0], where_ref[2], where_ref[4], where_ref[5]
    total, start = 0.0, 0
    for piece in pieces:
        size = piece.shape[0] * piece.shape[1]
        here = slice(start, start + size)
        left = jnp.concatenate([own_ref[:, here], other_ref[:, here], up_ref[:, here]], 0)
        total += jnp.dot(left, piece[...].reshape(size, 2 * rank), preferred_element_type=F32)
        start += size
    each = rows // 8
    for ref, begin in ((keep_ref, 0), (send_ref, rows)):
        for index in range(8):
            part = total[begin + index * each : begin + (index + 1) * each]
            ref[index * 2 * each : (index * 2 + 1) * each] = part[:, :rank]
            ref[(index * 2 + 1) * each : (index * 2 + 2) * each] = part[:, rank:]
    up_rows = up_ref.shape[0] // 8
    layers = []
    for layer in range(8):
        part = total[2 * rows + layer * up_rows : 2 * rows + (layer + 1) * up_rows]
        layers.append(jnp.where(layer < section, part[:, :rank], part[:, rank:]))
    low = jnp.concatenate(layers[:4], 0)
    high = jnp.concatenate(layers[4:], 0)
    keep_ref[2 * rows :] = jnp.where(core == 0, low, high)
    send_ref[2 * rows :] = jnp.where(core == 0, high, low)
    for index, piece in enumerate(pieces):
        for z in range(2):
            stay_ref[z * 4 + index] = piece[(zhi * 2 + z) ^ zlo, :, rank:]


def combine_kernel(keep_ref, came_ref, out_ref):
    sections, each, _ = out_ref.shape
    half = each // 2
    shared = keep_ref[sections * half :] + came_ref[sections * half :]
    for index in range(sections):
        here = slice(index * half, (index + 1) * half)
        out_ref[index, :half] = keep_ref[here] + came_ref[here]
        out_ref[index, half:] = shared


def gram_kernel(incoming_ref, out_ref):
    sections, each, rank = incoming_ref.shape
    for index in range(sections):
        out_ref[:, index * rank : (index + 1) * rank] = incoming_ref[index, each // 2 :].astype(
            BF16
        )


def chain_kernel(where_ref, products_ref, gram_ref, square_ref, sent_ref, latent_ref):
    layers, each, rank = products_ref.shape
    rows = each // 4
    width = where_ref[6].astype(F32)
    square = square_ref[...]
    for layer in range(layers):
        here = slice(layer * rank, (layer + 1) * rank)
        before = slice(0, layer * rank)
        entering = products_ref[layer, :rows]
        cross = products_ref[layer, rows : 2 * rows]
        if layer > 0:
            earlier = latent_ref[:, before]
            entering += jnp.dot(earlier, gram_ref[before, here], preferred_element_type=F32)
            cross += lax.dot_general(
                earlier,
                gram_ref[here, before],
                (((1,), (1,)), ((), ())),
                preferred_element_type=F32,
            )
        value = entering * lax.rsqrt(square / width + EPSILON)
        latent = (value / (1.0 + jnp.exp(-value))).astype(BF16)
        latent = jnp.where(layer <= where_ref[5], latent, jnp.zeros_like(latent))
        latent_ref[:, here] = latent
        spot = layer // 4 * 4 + gray(where_ref[1] ^ (layer % 4))
        sent_ref[:, pl.ds(pl.multiple_of(spot * rank, rank), rank)] = latent
        own = jnp.dot(latent, gram_ref[here, here], preferred_element_type=F32)
        grown = latent.astype(F32) * (2.0 * cross + own)
        square = jnp.maximum(square + jnp.sum(grown, -1, keepdims=True), 0.0)
    scale = lax.rsqrt(square / width + EPSILON)
    scale = jnp.broadcast_to(scale, (rows, rank))
    lane = lax.broadcasted_iota(jnp.int32, (rows, rank), 1)
    high = scale.astype(BF16).astype(F32)
    middle = (scale - high).astype(BF16).astype(F32)
    low = scale - high - middle
    parts = jnp.where(lane == 0, high, jnp.where(lane == 1, middle, low))
    parts = jnp.where(lane < 3, parts, 0.0)
    sent_ref[:, layers * rank :] = parts.astype(BF16)


def head_kernel(*refs):
    pieces, (head_ref, other_ref, out_ref) = refs[:-3], refs[-3:]
    left = jnp.concatenate([piece[...] for piece in pieces], 0)
    half = head_ref.shape[1]
    out_ref[:, :half] = jnp.dot(left, head_ref[...], preferred_element_type=F32).astype(
        out_ref.dtype
    )
    out_ref[:, half:] = jnp.dot(left, other_ref[...], preferred_element_type=F32).astype(
        out_ref.dtype
    )


def correction_kernel(where_ref, own_ref, *refs):
    came_refs, (head_ref, other_ref, keep_ref, send_ref) = refs[:4], refs[4:]
    blocks, block, rank = own_ref.shape
    half = head_ref.shape[1]
    zhi, x, y, core = where_ref[0], where_ref[1], where_ref[3], where_ref[4]
    totals = [0.0, 0.0]
    for index in range(blocks):
        at = index // 4 * 4 + (y ^ gray(index % 4))
        start = gray(x ^ (at // 2)) * 4 + at % 2 * 2 + core
        here = pl.ds(pl.multiple_of(start * block, block), block)
        maps = jnp.concatenate([own_ref[index], came_refs[index % 4][index // 4]], 1)
        for spot, ref in enumerate((head_ref, other_ref)):
            totals[spot] += lax.dot_general(
                maps, ref[here, :], (((0,), (0,)), ((), ())), preferred_element_type=F32
            )
    for spot, total in enumerate(totals):
        mine = jnp.where(core == zhi, total[:rank], total[rank:])
        theirs = jnp.where(core == zhi, total[rank:], total[:rank])
        keep_ref[:, spot * half : (spot + 1) * half] = mine
        send_ref[:, (1 - spot) * half : (2 - spot) * half] = theirs.astype(BF16)


def losses_kernel(
    where_ref, latents_ref, own_ref, other_ref, base_ref, came_ref, wanted_ref, out_ref
):
    zlo, y, core = where_ref[2], where_ref[3], where_ref[4]
    places = [(zlo ^ (index % 4)) * 4 + (y ^ gray(index // 4)) for index in range(16)]
    latents = jnp.concatenate([latents_ref[place] for place in places], 0)
    depth, columns = own_ref.shape
    half = columns // 2
    scale = jnp.sum(latents[:, 2 * depth :].astype(F32), -1, keepdims=True)
    low, high = latents[:, :depth], latents[:, depth : 2 * depth]
    mine = jnp.where(core == 0, low, high)
    theirs = jnp.where(core == 0, high, low)
    exp_total, picked = 0.0, 0.0
    for spot in range(2):
        here = slice(spot * half, (spot + 1) * half)
        there = slice((1 - spot) * half, (2 - spot) * half)
        logits = base_ref[:, here] + came_ref[:, here].astype(F32)
        logits += jnp.dot(mine, own_ref[:, here], preferred_element_type=F32)
        logits += jnp.dot(theirs, other_ref[:, there], preferred_element_type=F32)
        capped = LOGIT_CEILING * jnp.tanh(logits * scale * RECIPROCAL_HEAT / LOGIT_CEILING)
        exp_total += jnp.sum(jnp.exp(capped), -1, keepdims=True)
        begin = ((zlo * 4 + y) * 2 + (core ^ spot)) * half
        column = begin + lax.broadcasted_iota(jnp.int32, capped.shape, 1)
        picked += jnp.sum(jnp.where(column == wanted_ref[...], capped, 0.0), -1, keepdims=True)
    plane, each, lanes = out_ref.shape
    lane = lax.broadcasted_iota(jnp.int32, (plane * each, lanes), 1)
    sums = jnp.where(lane == 0, exp_total, jnp.where(lane == 1, picked, 0.0))
    for index, place in enumerate(places):
        out_ref[place] = sums[index * each : (index + 1) * each]


def finish_kernel(sums_ref, out_ref):
    total = sums_ref[0]
    for index in range(1, sums_ref.shape[0]):
        total += sums_ref[index]
    out_ref[...] = jnp.log(total[:, :1]) - total[:, 1:2]


def per_device(
    inputs, layer_gain, layer_down, layer_up, exit_norm_gain, head_weight, targets, exit_section
):
    section = lax.axis_index(SECTION)
    place = lax.axis_index(DP)
    zhi, x, zlo, y, core = (lax.axis_index(name) for name in SECTION + DP)
    micro, tokens, width = inputs.shape
    sections = lax.axis_size(SECTION)
    plane = lax.axis_size(PLANE)
    rank = layer_up.shape[1]
    own_rank = rank // plane
    exits = micro // sections
    rows = exits * tokens
    head_rows, head_columns = head_weight.shape
    where = jnp.stack([zhi, x, zlo, y, core, section, jnp.int32(width)]).astype(jnp.int32)

    head_gain = lax.dynamic_slice_in_dim(exit_norm_gain, section * head_rows, head_rows, 0)
    scaled_head = (head_weight.astype(F32) * head_gain[:, None]).astype(BF16)

    up = layer_up[0]
    features = up.shape[1]
    came = lax.all_to_all(up, PLANE, 0, 0, tiled=True).reshape(plane, own_rank, features)

    gain = lax.dynamic_slice_in_dim(layer_gain[0], place * features, features, 0)
    scaled_down = (layer_down[0].astype(F32) * gain[:, None]).astype(BF16)
    pair = jnp.concatenate([scaled_down, up.T], 1)
    lined = direct(pair, "zlo", LINE)

    half_rows = ((sections * rows, width // 2), BF16, "v")
    own_rows, other_rows, own_square, all_rows, wanted, _ = kernel_call(
        rows_kernel,
        [
            half_rows,
            half_rows,
            ((rows, 1), F32, "v"),
            ((sections * rows, width), BF16, "v"),
            ((plane * rows, 1), jnp.int32, "v"),
            ((micro,), jnp.int32, "s"),
        ],
        [where, tied(exit_section, came)],
        [inputs, targets],
        scratch=[pltpu.SMEM((sections,), jnp.int32)],
    )
    lined = stack([tied(piece, came)[None] for piece in lined])
    maps = direct(lined, "y", RING)

    (leaving,) = kernel_call(
        leaving_kernel, [((2, features, rank), BF16, "v")], [where], [lined]
    )
    up_came = hop(leaving, "zhi", 1)
    partner_rows = hop(tied(other_rows, up_came), "core", 1)

    (state,) = kernel_call(
        state_kernel, [((2 * rows, width // 2), BF16, "v")], [where], [all_rows]
    )
    state = tied(state, up_came)
    (state,) = kernel_call(
        pair_kernel, [((4 * rows, width // 2), BF16, "v")], [], [state, hop(state, "zlo", 1)]
    )
    state = [state, hop(state, "zlo", 2)]

    (copies,) = kernel_call(
        up_kernel, [((sections, own_rank, width // 2), BF16, "v")], [where], [came]
    )
    copies = tied(copies, up_came)
    up_rows = lax.all_to_all(copies, SECTION, 0, 0, tiled=True)
    up_rows = up_rows.reshape(sections * own_rank, width // 2)

    up_came = direct(tied(up_came, *maps), "y", RING)

    sums = ((2 * sections * rows + 4 * own_rank, rank), F32, "v")
    keep, send, up_stay = kernel_call(
        products_kernel,
        [sums, sums, ((plane // 2, features, rank), BF16, "v")],
        [where],
        [own_rows, partner_rows, up_rows, *maps],
    )
    (outgoing,) = kernel_call(
        combine_kernel, [((sections, 4 * rows, rank), F32, "v")], [], [keep, hop(send, "core", 1)]
    )
    head_pieces = direct(tied(scaled_head, up_rows), "x", RING)
    line_rows = ((4 * rows, width // 2), BF16, "v")
    state = kernel_call(part_kernel, [line_rows, line_rows], [], [tied(part, send) for part in state])
    passing, staying = ring(*state, "y")

    outgoing = tied(outgoing, *up_came, *state)
    incoming = lax.all_to_all(outgoing, SECTION, 0, 0, tiled=True)
    (gram,) = kernel_call(
        gram_kernel, [((4 * own_rank, sections * rank), BF16, "v")], [], [incoming]
    )
    gram = spread(tied(gram, *passing[1:3], *staying[1:3]), "zlo")
    gram = spread(tied(gram, passing[3], staying[3]), "y").reshape(-1, sections * rank)
    head = stack([tied(piece, incoming) for piece in head_pieces])
    other_head = hop(head, "core", 1)
    wide = 2 * head_columns
    mine, theirs = kernel_call(
        correction_kernel,
        [((rank, wide), F32, "v"), ((rank, wide), BF16, "v")],
        [where],
        [up_stay, *up_came, head, other_head],
    )
    mine = mine + hop(theirs, "core", 1).astype(F32)
    mine = (mine + hop(mine.astype(BF16), "zhi", 1).astype(F32)).astype(BF16)
    correction = direct(mine, "x", RING)

    def through(pieces, dtype):
        shape = (plane * rows, wide)
        return kernel_call(
            head_kernel, [(shape, dtype, "v")], [], [*pieces, head, other_head]
        )[0]

    passing = through(passing, BF16)
    passed = hop(passing, "zhi", 1)
    base = through(staying, F32)

    gram = tied(gram, mine, passing, staying[3])
    steps = jnp.arange(4, dtype=jnp.int32)
    at = ((steps[None, :] * 4 + steps[:, None]) * own_rank)[..., None, None]
    at = at + (steps * rank)[:, None] + jnp.arange(own_rank, dtype=jnp.int32)
    at = at.reshape(-1)
    line = jnp.arange(sections * rank, dtype=jnp.int32)[:, None]
    own_sorting = (line == (at + core * 4 * rank)[None, :]).astype(BF16)
    other_sorting = (line == (at + (1 - core) * 4 * rank)[None, :]).astype(BF16)
    gram = jnp.dot(own_sorting, gram, preferred_element_type=F32) + jnp.dot(
        other_sorting, hop(gram, "core", 1), preferred_element_type=F32
    )
    (latents,) = kernel_call(
        chain_kernel,
        [((rows, (sections + 1) * rank), BF16, "v")],
        [where],
        [incoming, gram.astype(BF16), own_square],
        scratch=[pltpu.VMEM((rows, sections * rank), BF16)],
    )

    latents = spread(tied(latents, passed, *correction), PLANE)
    correction = stack(correction)
    other_correction = hop(correction, "core", 1)
    (sums,) = kernel_call(
        losses_kernel,
        [((plane, rows, rank), F32, "v")],
        [where],
        [latents, correction, other_correction, base, passed, wanted],
    )
    sums = lax.all_to_all(sums, PLANE, 0, 0, tiled=True)
    (losses,) = kernel_call(finish_kernel, [((rows, 1), F32, "v")], [], [sums])
    return losses.reshape(1, exits, tokens)


def solution(mesh):
    split = Mesh(mesh.devices.reshape(2, 4, 4, 4, 2), SECTION + DP)
    placed = (
        P(None, DP, None),
        P(SECTION, None),
        P(SECTION, DP, None),
        P(SECTION, None, DP),
        P(),
        P(SECTION, DP),
        P(),
        P(),
    )
    return jax.shard_map(
        per_device, mesh=split, in_specs=placed, out_specs=P(SECTION, None, DP), check_vma=False
    )
```

```python
import math

import functools

import jax
import jax.numpy as jnp
from jax import lax
from jax.experimental import pallas as pl
from jax.experimental.pallas import tpu as pltpu
from jax.sharding import Mesh, PartitionSpec as P

EPSILON = 1e-05
LOGIT_CEILING = 30.0
RECIPROCAL_HEAT = 1.0 / 0.7
INTERPRET = False

SECTION = ("zhi", "x")
DP = ("zlo", "y", "core")
PLANE = ("zlo", "y")
LINE = (0, 1, 2, 3)
RING = (0, 1, 3, 2)
F32, BF16 = jnp.float32, jnp.bfloat16


def hop(block, axis, bit):
    size = lax.axis_size(axis)
    return lax.ppermute(block, axis, [(i, i ^ bit) for i in range(size)])


def ring(low, high, axis):
    three_low = hop(low, axis, 3)
    one_high = hop(high, axis, 1)
    one_low = hop(low, axis, 1)
    three_high = hop(high, axis, 3)
    far_low = hop(three_low, axis, 1)
    far_high = hop(one_high, axis, 3)
    return [low, one_low, three_low, far_low], [high, one_high, three_high, far_high]


def tied(value, *others):
    return lax.optimization_barrier((value, *others))[0]


def spread(block, axis):
    size = lax.axis_size(axis)
    copies = jnp.broadcast_to(block[None], (size, *block.shape))
    return lax.all_to_all(copies, axis, 0, 0, tiled=True)


def direct(block, axis, order):
    return [block] + [hop(block, axis, bit) for bit in order[1:]]


def kernel_call(body, out, scalars, arrays, after=(), scratch=()):
    whole = pl.BlockSpec(memory_space=pltpu.VMEM)
    small = pl.BlockSpec(memory_space=pltpu.SMEM)
    unread = pl.BlockSpec(memory_space=pl.ANY)
    count = len(scalars) + len(arrays)

    def inner(*refs):
        body(*refs[:count], *refs[count + len(after) :])

    shapes = [jax.ShapeDtypeStruct(shape, dtype) for shape, dtype, _ in out]
    sizes = [math.prod(one.shape) * one.dtype.itemsize for one in [*shapes, *arrays]]
    limit = 6 + 5 * sum(sizes) // 2**22
    return pl.pallas_call(
        inner,
        out_shape=shapes,
        in_specs=[small] * len(scalars) + [whole] * len(arrays) + [unread] * len(after),
        out_specs=[whole if space == "v" else small for _, _, space in out],
        scratch_shapes=list(scratch),
        compiler_params=pltpu.CompilerParams(vmem_limit_bytes=limit * 2**20),
        interpret=INTERPRET,
    )(*scalars, *arrays, *after)


def gray(value):
    return value ^ (value >> 1)


def stack_kernel(*refs):
    out_ref = refs[-1]
    start = 0
    for ref in refs[:-1]:
        out_ref[start : start + ref.shape[0]] = ref[...]
        start += ref.shape[0]


def stack(pieces):
    total = sum(piece.shape[0] for piece in pieces)
    shape = (total, *pieces[0].shape[1:])
    return kernel_call(stack_kernel, [(shape, pieces[0].dtype, "v")], [], pieces)[0]


def block_at(where_ref, index):
    return (where_ref[2] ^ (index % 4)) * 4 + (where_ref[3] ^ gray(index // 4))


def rows_kernel(
    where_ref,
    exits_ref,
    inputs_ref,
    targets_ref,
    own_ref,
    other_ref,
    square_ref,
    rows_ref,
    wanted_ref,
    chosen_ref,
    count_ref,
):
    micro, tokens, width = inputs_ref.shape
    sections = 8
    exits = micro // sections
    each = exits * tokens
    zlo, y, core, section = where_ref[2], where_ref[3], where_ref[4], where_ref[5]
    for index in range(sections):
        count_ref[index] = 0
    for index in range(micro):
        place = exits_ref[index]
        spot = count_ref[place]
        count_ref[place] = spot + 1
        chosen_ref[place * exits + spot] = index
    for place in range(sections):
        parts = [inputs_ref[chosen_ref[place * exits + spot]].astype(F32) for spot in range(exits)]
        rows_ref[place * each : (place + 1) * each, :] = jnp.concatenate(parts, 0).astype(BF16)
    own = rows_ref[pl.ds(pl.multiple_of(section * each, each), each), :].astype(F32)
    square_ref[...] = jnp.sum(own * own, -1, keepdims=True)
    block = width // 32
    for index in range(16):
        start = block_at(where_ref, index) * 2 * block
        here = slice(index * block, (index + 1) * block)
        mine = pl.multiple_of(start + core * block, block)
        theirs = pl.multiple_of(start + (1 - core) * block, block)
        own_ref[:, here] = rows_ref[:, pl.ds(mine, block)]
        other_ref[:, here] = rows_ref[:, pl.ds(theirs, block)]
    lanes = targets_ref.shape[1]
    ids = [
        jnp.broadcast_to(targets_ref[pl.ds(chosen_ref[section * exits + spot], 1), :], (tokens, lanes))
        for spot in range(exits)
    ]
    ids = jnp.concatenate(ids * 16, 0)
    row = lax.broadcasted_iota(jnp.int32, ids.shape, 0)
    lane = lax.broadcasted_iota(jnp.int32, ids.shape, 1)
    ring_step = row // (4 * each)
    from_y = y ^ gray(ring_step)
    from_z = zlo ^ (row // each % 4)
    token = ((from_z * 4 + from_y) * 2 + core) * tokens + row % tokens
    wanted_ref[...] = jnp.sum(jnp.where(lane == token, ids, 0), -1, keepdims=True)


def state_kernel(where_ref, rows_ref, out_ref):
    each = out_ref.shape[0] // 2
    quarter = out_ref.shape[1] // 4
    zhi, x = where_ref[0], where_ref[1]
    for spot, half in ((0, 1 - zhi), (1, zhi)):
        begin = pl.multiple_of((half * 4 + x) * each, each)
        for index in range(4):
            start = pl.multiple_of((zhi * 4 + (x ^ gray(index))) * quarter, quarter)
            out_ref[spot * each : (spot + 1) * each, index * quarter : (index + 1) * quarter] = (
                rows_ref[pl.ds(begin, each), pl.ds(start, quarter)]
            )


def pair_kernel(first_ref, second_ref, out_ref):
    each = first_ref.shape[0] // 2
    out_ref[:each] = first_ref[:each]
    out_ref[each : 2 * each] = second_ref[:each]
    out_ref[2 * each : 3 * each] = first_ref[each:]
    out_ref[3 * each :] = second_ref[each:]


def part_kernel(first_ref, second_ref, low_ref, high_ref):
    each = first_ref.shape[0] // 2
    low_ref[:each] = first_ref[:each]
    low_ref[each:] = second_ref[:each]
    high_ref[:each] = first_ref[each:]
    high_ref[each:] = second_ref[each:]


def up_kernel(where_ref, came_ref, out_ref):
    block = came_ref.shape[2]
    for index in range(came_ref.shape[0]):
        piece = came_ref[block_at(where_ref, index)]
        for copy in range(out_ref.shape[0]):
            out_ref[copy, :, index * block : (index + 1) * block] = piece


def leaving_kernel(where_ref, lined_ref, out_ref):
    for z in range(2):
        at = ((1 - where_ref[0]) * 2 + z) ^ where_ref[2]
        out_ref[z] = lined_ref[at, :, out_ref.shape[2] :]


def products_kernel(where_ref, own_ref, other_ref, up_ref, *refs):
    pieces, (keep_ref, send_ref, stay_ref) = refs[:-3], refs[-3:]
    rows = own_ref.shape[0]
    rank = keep_ref.shape[1]
    zhi, zlo, core, section = where_ref[0], where_ref[2], where_ref[4], where_ref[5]
    total, start = 0.0, 0
    for piece in pieces:
        size = piece.shape[0] * piece.shape[1]
        here = slice(start, start + size)
        left = jnp.concatenate([own_ref[:, here], other_ref[:, here], up_ref[:, here]], 0)
        total += jnp.dot(left, piece[...].reshape(size, 2 * rank), preferred_element_type=F32)
        start += size
    each = rows // 8
    for ref, begin in ((keep_ref, 0), (send_ref, rows)):
        for index in range(8):
            part = total[begin + index * each : begin + (index + 1) * each]
            ref[index * 2 * each : (index * 2 + 1) * each] = part[:, :rank]
            ref[(index * 2 + 1) * each : (index * 2 + 2) * each] = part[:, rank:]
    up_rows = up_ref.shape[0] // 8
    layers = []
    for layer in range(8):
        part = total[2 * rows + layer * up_rows : 2 * rows + (layer + 1) * up_rows]
        layers.append(jnp.where(layer < section, part[:, :rank], part[:, rank:]))
    low = jnp.concatenate(layers[:4], 0)
    high = jnp.concatenate(layers[4:], 0)
    keep_ref[2 * rows :] = jnp.where(core == 0, low, high)
    send_ref[2 * rows :] = jnp.where(core == 0, high, low)
    for index, piece in enumerate(pieces):
        for z in range(2):
            stay_ref[z * 4 + index] = piece[(zhi * 2 + z) ^ zlo, :, rank:]


def combine_kernel(keep_ref, came_ref, out_ref):
    sections, each, _ = out_ref.shape
    half = each // 2
    shared = keep_ref[sections * half :] + came_ref[sections * half :]
    for index in range(sections):
        here = slice(index * half, (index + 1) * half)
        out_ref[index, :half] = keep_ref[here] + came_ref[here]
        out_ref[index, half:] = shared


def gram_kernel(incoming_ref, out_ref):
    sections, each, rank = incoming_ref.shape
    for index in range(sections):
        out_ref[:, index * rank : (index + 1) * rank] = incoming_ref[index, each // 2 :].astype(
            BF16
        )


def chain_kernel(
    where_ref, products_ref, own_ref, other_ref, square_ref, sent_ref, latent_ref, gram_ref
):
    layers, each, rank = products_ref.shape
    half = own_ref.shape[0]

    @pl.when(where_ref[4] == 0)
    def _():
        gram_ref[:half] = own_ref[...]
        gram_ref[half:] = other_ref[...]

    @pl.when(where_ref[4] != 0)
    def _():
        gram_ref[:half] = other_ref[...]
        gram_ref[half:] = own_ref[...]

    rows = each // 4
    width = where_ref[6].astype(F32)
    square = square_ref[...]
    for layer in range(layers):
        here = slice(layer * rank, (layer + 1) * rank)
        before = slice(0, layer * rank)
        entering = products_ref[layer, :rows]
        cross = products_ref[layer, rows : 2 * rows]
        if layer > 0:
            earlier = latent_ref[:, before]
            entering += jnp.dot(earlier, gram_ref[before, here], preferred_element_type=F32)
            cross += lax.dot_general(
                earlier,
                gram_ref[here, before],
                (((1,), (1,)), ((), ())),
                preferred_element_type=F32,
            )
        value = entering * lax.rsqrt(square / width + EPSILON)
        latent = (value / (1.0 + jnp.exp(-value))).astype(BF16)
        latent = jnp.where(layer <= where_ref[5], latent, jnp.zeros_like(latent))
        latent_ref[:, here] = latent
        spot = layer // 4 * 4 + gray(where_ref[1] ^ (layer % 4))
        sent_ref[:, pl.ds(pl.multiple_of(spot * rank, rank), rank)] = latent
        own = jnp.dot(latent, gram_ref[here, here], preferred_element_type=F32)
        grown = latent.astype(F32) * (2.0 * cross + own)
        square = jnp.maximum(square + jnp.sum(grown, -1, keepdims=True), 0.0)
    scale = lax.rsqrt(square / width + EPSILON)
    scale = jnp.broadcast_to(scale, (rows, rank))
    lane = lax.broadcasted_iota(jnp.int32, (rows, rank), 1)
    high = scale.astype(BF16).astype(F32)
    middle = (scale - high).astype(BF16).astype(F32)
    low = scale - high - middle
    parts = jnp.where(lane == 0, high, jnp.where(lane == 1, middle, low))
    parts = jnp.where(lane < 3, parts, 0.0)
    sent_ref[:, layers * rank :] = parts.astype(BF16)


def head_kernel(*refs):
    pieces, (head_ref, other_ref, out_ref) = refs[:-3], refs[-3:]
    left = jnp.concatenate([piece[...] for piece in pieces], 0)
    half = head_ref.shape[1]
    out_ref[:, :half] = jnp.dot(left, head_ref[...], preferred_element_type=F32).astype(
        out_ref.dtype
    )
    out_ref[:, half:] = jnp.dot(left, other_ref[...], preferred_element_type=F32).astype(
        out_ref.dtype
    )


def correction_kernel(where_ref, own_ref, *refs):
    came_refs, (head_ref, other_ref, keep_ref, send_ref) = refs[:4], refs[4:]
    blocks, block, rank = own_ref.shape
    half = head_ref.shape[1]
    zhi, x, y, core = where_ref[0], where_ref[1], where_ref[3], where_ref[4]
    totals = [0.0, 0.0]
    for index in range(blocks):
        at = index // 4 * 4 + (y ^ gray(index % 4))
        start = gray(x ^ (at // 2)) * 4 + at % 2 * 2 + core
        here = pl.ds(pl.multiple_of(start * block, block), block)
        maps = jnp.concatenate([own_ref[index], came_refs[index % 4][index // 4]], 1)
        for spot, ref in enumerate((head_ref, other_ref)):
            totals[spot] += lax.dot_general(
                maps, ref[here, :], (((0,), (0,)), ((), ())), preferred_element_type=F32
            )
    for spot, total in enumerate(totals):
        mine = jnp.where(core == zhi, total[:rank], total[rank:])
        theirs = jnp.where(core == zhi, total[rank:], total[:rank])
        keep_ref[:, spot * half : (spot + 1) * half] = mine
        send_ref[:, (1 - spot) * half : (2 - spot) * half] = theirs.astype(BF16)


def losses_kernel(
    where_ref, latents_ref, own_ref, other_ref, base_ref, came_ref, wanted_ref, out_ref
):
    zlo, y, core = where_ref[2], where_ref[3], where_ref[4]
    places = [(zlo ^ (index % 4)) * 4 + (y ^ gray(index // 4)) for index in range(16)]
    latents = jnp.concatenate([latents_ref[place] for place in places], 0)
    depth, columns = own_ref.shape
    half = columns // 2
    scale = jnp.sum(latents[:, 2 * depth :].astype(F32), -1, keepdims=True)
    low, high = latents[:, :depth], latents[:, depth : 2 * depth]
    mine = jnp.where(core == 0, low, high)
    theirs = jnp.where(core == 0, high, low)
    exp_total, picked = 0.0, 0.0
    for spot in range(2):
        here = slice(spot * half, (spot + 1) * half)
        there = slice((1 - spot) * half, (2 - spot) * half)
        logits = base_ref[:, here] + came_ref[:, here].astype(F32)
        logits += jnp.dot(mine, own_ref[:, here], preferred_element_type=F32)
        logits += jnp.dot(theirs, other_ref[:, there], preferred_element_type=F32)
        capped = LOGIT_CEILING * jnp.tanh(logits * scale * RECIPROCAL_HEAT / LOGIT_CEILING)
        exp_total += jnp.sum(jnp.exp(capped), -1, keepdims=True)
        begin = ((zlo * 4 + y) * 2 + (core ^ spot)) * half
        column = begin + lax.broadcasted_iota(jnp.int32, capped.shape, 1)
        picked += jnp.sum(jnp.where(column == wanted_ref[...], capped, 0.0), -1, keepdims=True)
    plane, each, lanes = out_ref.shape
    lane = lax.broadcasted_iota(jnp.int32, (plane * each, lanes), 1)
    sums = jnp.where(lane == 0, exp_total, jnp.where(lane == 1, picked, 0.0))
    for index, place in enumerate(places):
        out_ref[place] = sums[index * each : (index + 1) * each]


def finish_kernel(sums_ref, out_ref):
    total = sums_ref[0]
    for index in range(1, sums_ref.shape[0]):
        total += sums_ref[index]
    out_ref[...] = jnp.log(total[:, :1]) - total[:, 1:2]


def per_device(
    inputs, layer_gain, layer_down, layer_up, exit_norm_gain, head_weight, targets, exit_section
):
    section = lax.axis_index(SECTION)
    place = lax.axis_index(DP)
    zhi, x, zlo, y, core = (lax.axis_index(name) for name in SECTION + DP)
    micro, tokens, width = inputs.shape
    sections = lax.axis_size(SECTION)
    plane = lax.axis_size(PLANE)
    rank = layer_up.shape[1]
    own_rank = rank // plane
    exits = micro // sections
    rows = exits * tokens
    head_rows, head_columns = head_weight.shape
    where = jnp.stack([zhi, x, zlo, y, core, section, jnp.int32(width)]).astype(jnp.int32)

    head_gain = lax.dynamic_slice_in_dim(exit_norm_gain, section * head_rows, head_rows, 0)
    scaled_head = (head_weight.astype(F32) * head_gain[:, None]).astype(BF16)

    up = layer_up[0]
    features = up.shape[1]
    came = lax.all_to_all(up, PLANE, 0, 0, tiled=True).reshape(plane, own_rank, features)

    gain = lax.dynamic_slice_in_dim(layer_gain[0], place * features, features, 0)
    scaled_down = (layer_down[0].astype(F32) * gain[:, None]).astype(BF16)
    pair = jnp.concatenate([scaled_down, up.T], 1)
    lined = direct(pair, "zlo", LINE)

    half_rows = ((sections * rows, width // 2), BF16, "v")
    own_rows, other_rows, own_square, all_rows, wanted, _ = kernel_call(
        rows_kernel,
        [
            half_rows,
            half_rows,
            ((rows, 1), F32, "v"),
            ((sections * rows, width), BF16, "v"),
            ((plane * rows, 1), jnp.int32, "v"),
            ((micro,), jnp.int32, "s"),
        ],
        [where, tied(exit_section, came)],
        [inputs, targets],
        scratch=[pltpu.SMEM((sections,), jnp.int32)],
    )
    lined = stack([tied(piece, came)[None] for piece in lined])
    maps = direct(lined, "y", RING)

    (leaving,) = kernel_call(
        leaving_kernel, [((2, features, rank), BF16, "v")], [where], [lined]
    )
    up_came = hop(leaving, "zhi", 1)
    partner_rows = hop(tied(other_rows, up_came), "core", 1)

    (state,) = kernel_call(
        state_kernel, [((2 * rows, width // 2), BF16, "v")], [where], [all_rows]
    )
    state = tied(state, up_came)
    (state,) = kernel_call(
        pair_kernel, [((4 * rows, width // 2), BF16, "v")], [], [state, hop(state, "zlo", 1)]
    )
    state = [state, hop(state, "zlo", 2)]

    (copies,) = kernel_call(
        up_kernel, [((sections, own_rank, width // 2), BF16, "v")], [where], [came]
    )
    copies = tied(copies, up_came)
    up_rows = lax.all_to_all(copies, SECTION, 0, 0, tiled=True)
    up_rows = up_rows.reshape(sections * own_rank, width // 2)

    up_came = direct(tied(up_came, *maps), "y", RING)

    sums = ((2 * sections * rows + 4 * own_rank, rank), F32, "v")
    keep, send, up_stay = kernel_call(
        products_kernel,
        [sums, sums, ((plane // 2, features, rank), BF16, "v")],
        [where],
        [own_rows, partner_rows, up_rows, *maps],
    )
    (outgoing,) = kernel_call(
        combine_kernel, [((sections, 4 * rows, rank), F32, "v")], [], [keep, hop(send, "core", 1)]
    )
    head_pieces = direct(tied(scaled_head, up_rows), "x", RING)
    line_rows = ((4 * rows, width // 2), BF16, "v")
    state = kernel_call(part_kernel, [line_rows, line_rows], [], [tied(part, send) for part in state])
    passing, staying = ring(*state, "y")

    outgoing = tied(outgoing, *up_came, *state)
    incoming = lax.all_to_all(outgoing, SECTION, 0, 0, tiled=True)
    (gram,) = kernel_call(
        gram_kernel, [((4 * own_rank, sections * rank), BF16, "v")], [], [incoming]
    )
    gram = spread(tied(gram, *passing[1:3], *staying[1:3]), "zlo")
    gram = spread(tied(gram, passing[3], staying[3]), "y").reshape(-1, sections * rank)
    head = stack([tied(piece, outgoing) for piece in head_pieces])
    other_head = hop(head, "core", 1)
    wide = 2 * head_columns
    mine, theirs = kernel_call(
        correction_kernel,
        [((rank, wide), F32, "v"), ((rank, wide), BF16, "v")],
        [where],
        [up_stay, *up_came, head, other_head],
    )
    mine = mine + hop(theirs, "core", 1).astype(F32)
    mine = (mine + hop(mine.astype(BF16), "zhi", 1).astype(F32)).astype(BF16)
    correction = direct(mine, "x", RING)

    def through(pieces, dtype):
        shape = (plane * rows, wide)
        return kernel_call(
            head_kernel, [(shape, dtype, "v")], [], [*pieces, head, other_head]
        )[0]

    passing = through(passing, BF16)
    passed = hop(passing, "zhi", 1)
    base = through(staying, F32)

    gram = tied(gram, mine, passing, staying[3])
    steps = jnp.arange(4, dtype=jnp.int32)
    at = ((steps[None, :] * 4 + steps[:, None]) * own_rank)[..., None, None]
    at = at + (steps * rank)[:, None] + jnp.arange(own_rank, dtype=jnp.int32)
    line = jnp.arange(4 * rank, dtype=jnp.int32)[:, None]
    sorting = (line == at.reshape(1, -1)).astype(BF16)
    gram = jnp.dot(sorting, gram, preferred_element_type=F32).astype(BF16)
    partner_gram = hop(gram, "core", 1)
    (latents,) = kernel_call(
        chain_kernel,
        [((rows, (sections + 1) * rank), BF16, "v")],
        [where],
        [incoming, gram, partner_gram, own_square],
        scratch=[
            pltpu.VMEM((rows, sections * rank), BF16),
            pltpu.VMEM((sections * rank, sections * rank), BF16),
        ],
    )

    latents = spread(tied(latents, passed, *correction), PLANE)
    correction = stack(correction)
    other_correction = hop(correction, "core", 1)
    (sums,) = kernel_call(
        losses_kernel,
        [((plane, rows, rank), F32, "v")],
        [where],
        [latents, correction, other_correction, base, passed, wanted],
    )
    sums = lax.all_to_all(sums, PLANE, 0, 0, tiled=True)
    (losses,) = kernel_call(finish_kernel, [((rows, 1), F32, "v")], [], [sums])
    return losses.reshape(1, exits, tokens)


def solution(mesh):
    split = Mesh(mesh.devices.reshape(2, 4, 4, 4, 2), SECTION + DP)
    placed = (
        P(None, DP, None),
        P(SECTION, None),
        P(SECTION, DP, None),
        P(SECTION, None, DP),
        P(),
        P(SECTION, DP),
        P(),
        P(),
    )
    return jax.shard_map(
        per_device, mesh=split, in_specs=placed, out_specs=P(SECTION, None, DP), check_vma=False
    )
```

```python
import math

import functools

import jax
import jax.numpy as jnp
from jax import lax
from jax.experimental import pallas as pl
from jax.experimental.pallas import tpu as pltpu
from jax.sharding import Mesh, PartitionSpec as P

EPSILON = 1e-05
LOGIT_CEILING = 30.0
RECIPROCAL_HEAT = 1.0 / 0.7
INTERPRET = False

SECTION = ("zhi", "x")
DP = ("zlo", "y", "core")
PLANE = ("zlo", "y")
LINE = (0, 1, 2, 3)
RING = (0, 1, 3, 2)
F32, BF16 = jnp.float32, jnp.bfloat16


def hop(block, axis, bit):
    size = lax.axis_size(axis)
    return lax.ppermute(block, axis, [(i, i ^ bit) for i in range(size)])


def ring(low, high, axis):
    three_low = hop(low, axis, 3)
    one_high = hop(high, axis, 1)
    one_low = hop(low, axis, 1)
    three_high = hop(high, axis, 3)
    far_low = hop(three_low, axis, 1)
    far_high = hop(one_high, axis, 3)
    return [low, one_low, three_low, far_low], [high, one_high, three_high, far_high]


def tied(value, *others):
    return lax.optimization_barrier((value, *others))[0]


def spread(block, axis):
    size = lax.axis_size(axis)
    copies = jnp.broadcast_to(block[None], (size, *block.shape))
    return lax.all_to_all(copies, axis, 0, 0, tiled=True)


def direct(block, axis, order):
    return [block] + [hop(block, axis, bit) for bit in order[1:]]


def kernel_call(body, out, scalars, arrays, after=(), scratch=()):
    whole = pl.BlockSpec(memory_space=pltpu.VMEM)
    small = pl.BlockSpec(memory_space=pltpu.SMEM)
    unread = pl.BlockSpec(memory_space=pl.ANY)
    count = len(scalars) + len(arrays)

    def inner(*refs):
        body(*refs[:count], *refs[count + len(after) :])

    shapes = [jax.ShapeDtypeStruct(shape, dtype) for shape, dtype, _ in out]
    sizes = [math.prod(one.shape) * one.dtype.itemsize for one in [*shapes, *arrays]]
    limit = 6 + 5 * sum(sizes) // 2**22
    return pl.pallas_call(
        inner,
        out_shape=shapes,
        in_specs=[small] * len(scalars) + [whole] * len(arrays) + [unread] * len(after),
        out_specs=[whole if space == "v" else small for _, _, space in out],
        scratch_shapes=list(scratch),
        compiler_params=pltpu.CompilerParams(vmem_limit_bytes=limit * 2**20),
        interpret=INTERPRET,
    )(*scalars, *arrays, *after)


def gray(value):
    return value ^ (value >> 1)


def stack_kernel(*refs):
    out_ref = refs[-1]
    start = 0
    for ref in refs[:-1]:
        out_ref[start : start + ref.shape[0]] = ref[...]
        start += ref.shape[0]


def stack(pieces):
    total = sum(piece.shape[0] for piece in pieces)
    shape = (total, *pieces[0].shape[1:])
    return kernel_call(stack_kernel, [(shape, pieces[0].dtype, "v")], [], pieces)[0]


def block_at(where_ref, index):
    return (where_ref[2] ^ (index % 4)) * 4 + (where_ref[3] ^ gray(index // 4))


def rows_kernel(
    where_ref,
    exits_ref,
    inputs_ref,
    targets_ref,
    own_ref,
    other_ref,
    square_ref,
    rows_ref,
    wanted_ref,
    chosen_ref,
    count_ref,
):
    micro, tokens, width = inputs_ref.shape
    sections = 8
    exits = micro // sections
    each = exits * tokens
    zlo, y, core, section = where_ref[2], where_ref[3], where_ref[4], where_ref[5]
    for index in range(sections):
        count_ref[index] = 0
    for index in range(micro):
        place = exits_ref[index]
        spot = count_ref[place]
        count_ref[place] = spot + 1
        chosen_ref[place * exits + spot] = index
    for place in range(sections):
        parts = [inputs_ref[chosen_ref[place * exits + spot]].astype(F32) for spot in range(exits)]
        rows_ref[place * each : (place + 1) * each, :] = jnp.concatenate(parts, 0).astype(BF16)
    own = rows_ref[pl.ds(pl.multiple_of(section * each, each), each), :].astype(F32)
    square_ref[...] = jnp.sum(own * own, -1, keepdims=True)
    block = width // 32
    for index in range(16):
        start = block_at(where_ref, index) * 2 * block
        here = slice(index * block, (index + 1) * block)
        mine = pl.multiple_of(start + core * block, block)
        theirs = pl.multiple_of(start + (1 - core) * block, block)
        own_ref[:, here] = rows_ref[:, pl.ds(mine, block)]
        other_ref[:, here] = rows_ref[:, pl.ds(theirs, block)]
    lanes = targets_ref.shape[1]
    ids = [
        jnp.broadcast_to(targets_ref[pl.ds(chosen_ref[section * exits + spot], 1), :], (tokens, lanes))
        for spot in range(exits)
    ]
    ids = jnp.concatenate(ids * 16, 0)
    row = lax.broadcasted_iota(jnp.int32, ids.shape, 0)
    lane = lax.broadcasted_iota(jnp.int32, ids.shape, 1)
    ring_step = row // (4 * each)
    from_y = y ^ gray(ring_step)
    from_z = zlo ^ (row // each % 4)
    token = ((from_z * 4 + from_y) * 2 + core) * tokens + row % tokens
    wanted_ref[...] = jnp.sum(jnp.where(lane == token, ids, 0), -1, keepdims=True)


def state_kernel(where_ref, rows_ref, out_ref):
    each = out_ref.shape[0] // 2
    quarter = out_ref.shape[1] // 4
    zhi, x = where_ref[0], where_ref[1]
    for spot, half in ((0, 1 - zhi), (1, zhi)):
        begin = pl.multiple_of((half * 4 + x) * each, each)
        for index in range(4):
            start = pl.multiple_of((zhi * 4 + (x ^ gray(index))) * quarter, quarter)
            out_ref[spot * each : (spot + 1) * each, index * quarter : (index + 1) * quarter] = (
                rows_ref[pl.ds(begin, each), pl.ds(start, quarter)]
            )


def pair_kernel(first_ref, second_ref, out_ref):
    each = first_ref.shape[0] // 2
    out_ref[:each] = first_ref[:each]
    out_ref[each : 2 * each] = second_ref[:each]
    out_ref[2 * each : 3 * each] = first_ref[each:]
    out_ref[3 * each :] = second_ref[each:]


def part_kernel(first_ref, second_ref, low_ref, high_ref):
    each = first_ref.shape[0] // 2
    low_ref[:each] = first_ref[:each]
    low_ref[each:] = second_ref[:each]
    high_ref[:each] = first_ref[each:]
    high_ref[each:] = second_ref[each:]


def up_kernel(where_ref, came_ref, out_ref):
    block = came_ref.shape[2]
    for index in range(came_ref.shape[0]):
        piece = came_ref[block_at(where_ref, index)]
        for copy in range(out_ref.shape[0]):
            out_ref[copy, :, index * block : (index + 1) * block] = piece


def leaving_kernel(where_ref, lined_ref, out_ref):
    for z in range(2):
        at = ((1 - where_ref[0]) * 2 + z) ^ where_ref[2]
        out_ref[z] = lined_ref[at, :, out_ref.shape[2] :]


def products_kernel(where_ref, own_ref, other_ref, up_ref, *refs):
    pieces, (keep_ref, send_ref, stay_ref) = refs[:-3], refs[-3:]
    rows = own_ref.shape[0]
    rank = keep_ref.shape[1]
    zhi, zlo, core, section = where_ref[0], where_ref[2], where_ref[4], where_ref[5]
    total, start = 0.0, 0
    for piece in pieces:
        size = piece.shape[0] * piece.shape[1]
        here = slice(start, start + size)
        left = jnp.concatenate([own_ref[:, here], other_ref[:, here], up_ref[:, here]], 0)
        total += jnp.dot(left, piece[...].reshape(size, 2 * rank), preferred_element_type=F32)
        start += size
    each = rows // 8
    for ref, begin in ((keep_ref, 0), (send_ref, rows)):
        for index in range(8):
            part = total[begin + index * each : begin + (index + 1) * each]
            ref[index * 2 * each : (index * 2 + 1) * each] = part[:, :rank]
            ref[(index * 2 + 1) * each : (index * 2 + 2) * each] = part[:, rank:]
    up_rows = up_ref.shape[0] // 8
    layers = []
    for layer in range(8):
        part = total[2 * rows + layer * up_rows : 2 * rows + (layer + 1) * up_rows]
        layers.append(jnp.where(layer < section, part[:, :rank], part[:, rank:]))
    low = jnp.concatenate(layers[:4], 0)
    high = jnp.concatenate(layers[4:], 0)
    keep_ref[2 * rows :] = jnp.where(core == 0, low, high)
    send_ref[2 * rows :] = jnp.where(core == 0, high, low)
    for index, piece in enumerate(pieces):
        for z in range(2):
            stay_ref[z * 4 + index] = piece[(zhi * 2 + z) ^ zlo, :, rank:]


def combine_kernel(keep_ref, came_ref, out_ref):
    sections, each, _ = out_ref.shape
    half = each // 2
    shared = keep_ref[sections * half :] + came_ref[sections * half :]
    for index in range(sections):
        here = slice(index * half, (index + 1) * half)
        out_ref[index, :half] = keep_ref[here] + came_ref[here]
        out_ref[index, half:] = shared


def gram_kernel(incoming_ref, out_ref):
    sections, each, rank = incoming_ref.shape
    for index in range(sections):
        out_ref[:, index * rank : (index + 1) * rank] = incoming_ref[index, each // 2 :].astype(
            BF16
        )


def chain_kernel(
    where_ref, products_ref, own_ref, other_ref, square_ref, sent_ref, latent_ref, gram_ref
):
    layers, each, rank = products_ref.shape
    half = own_ref.shape[0]

    @pl.when(where_ref[4] == 0)
    def _():
        gram_ref[:half] = own_ref[...]
        gram_ref[half:] = other_ref[...]

    @pl.when(where_ref[4] != 0)
    def _():
        gram_ref[:half] = other_ref[...]
        gram_ref[half:] = own_ref[...]

    rows = each // 4
    width = where_ref[6].astype(F32)
    square = square_ref[...]
    for layer in range(layers):
        here = slice(layer * rank, (layer + 1) * rank)
        before = slice(0, layer * rank)
        entering = products_ref[layer, :rows]
        cross = products_ref[layer, rows : 2 * rows]
        if layer > 0:
            earlier = latent_ref[:, before]
            entering += jnp.dot(earlier, gram_ref[before, here], preferred_element_type=F32)
            cross += lax.dot_general(
                earlier,
                gram_ref[here, before],
                (((1,), (1,)), ((), ())),
                preferred_element_type=F32,
            )
        value = entering * lax.rsqrt(square / width + EPSILON)
        latent = (value / (1.0 + jnp.exp(-value))).astype(BF16)
        latent = jnp.where(layer <= where_ref[5], latent, jnp.zeros_like(latent))
        latent_ref[:, here] = latent
        spot = layer // 4 * 4 + gray(where_ref[1] ^ (layer % 4))
        sent_ref[:, pl.ds(pl.multiple_of(spot * rank, rank), rank)] = latent
        own = jnp.dot(latent, gram_ref[here, here], preferred_element_type=F32)
        grown = latent.astype(F32) * (2.0 * cross + own)
        square = jnp.maximum(square + jnp.sum(grown, -1, keepdims=True), 0.0)
    scale = lax.rsqrt(square / width + EPSILON)
    scale = jnp.broadcast_to(scale, (rows, rank))
    lane = lax.broadcasted_iota(jnp.int32, (rows, rank), 1)
    high = scale.astype(BF16).astype(F32)
    middle = (scale - high).astype(BF16).astype(F32)
    low = scale - high - middle
    parts = jnp.where(lane == 0, high, jnp.where(lane == 1, middle, low))
    parts = jnp.where(lane < 3, parts, 0.0)
    sent_ref[:, layers * rank :] = parts.astype(BF16)


def head_kernel(*refs):
    pieces, (head_ref, other_ref, out_ref) = refs[:-3], refs[-3:]
    left = jnp.concatenate([piece[...] for piece in pieces], 0)
    half = head_ref.shape[1]
    out_ref[:, :half] = jnp.dot(left, head_ref[...], preferred_element_type=F32).astype(
        out_ref.dtype
    )
    out_ref[:, half:] = jnp.dot(left, other_ref[...], preferred_element_type=F32).astype(
        out_ref.dtype
    )


def correction_kernel(where_ref, own_ref, *refs):
    came_refs, (head_ref, other_ref, keep_ref, send_ref) = refs[:4], refs[4:]
    blocks, block, rank = own_ref.shape
    half = head_ref.shape[1]
    zhi, x, y, core = where_ref[0], where_ref[1], where_ref[3], where_ref[4]
    totals = [0.0, 0.0]
    for index in range(blocks):
        at = index // 4 * 4 + (y ^ gray(index % 4))
        start = gray(x ^ (at // 2)) * 4 + at % 2 * 2 + core
        here = pl.ds(pl.multiple_of(start * block, block), block)
        maps = jnp.concatenate([own_ref[index], came_refs[index % 4][index // 4]], 1)
        for spot, ref in enumerate((head_ref, other_ref)):
            totals[spot] += lax.dot_general(
                maps, ref[here, :], (((0,), (0,)), ((), ())), preferred_element_type=F32
            )
    for spot, total in enumerate(totals):
        mine = jnp.where(core == zhi, total[:rank], total[rank:])
        theirs = jnp.where(core == zhi, total[rank:], total[:rank])
        keep_ref[:, spot * half : (spot + 1) * half] = mine
        send_ref[:, (1 - spot) * half : (2 - spot) * half] = theirs.astype(BF16)


def losses_kernel(
    where_ref, latents_ref, own_ref, other_ref, base_ref, came_ref, wanted_ref, out_ref
):
    zlo, y, core = where_ref[2], where_ref[3], where_ref[4]
    places = [(zlo ^ (index % 4)) * 4 + (y ^ gray(index // 4)) for index in range(16)]
    latents = jnp.concatenate([latents_ref[place] for place in places], 0)
    depth, columns = own_ref.shape
    half = columns // 2
    scale = jnp.sum(latents[:, 2 * depth :].astype(F32), -1, keepdims=True)
    low, high = latents[:, :depth], latents[:, depth : 2 * depth]
    mine = jnp.where(core == 0, low, high)
    theirs = jnp.where(core == 0, high, low)
    exp_total, picked = 0.0, 0.0
    for spot in range(2):
        here = slice(spot * half, (spot + 1) * half)
        there = slice((1 - spot) * half, (2 - spot) * half)
        logits = base_ref[:, here] + came_ref[:, here].astype(F32)
        logits += jnp.dot(mine, own_ref[:, here], preferred_element_type=F32)
        logits += jnp.dot(theirs, other_ref[:, there], preferred_element_type=F32)
        capped = LOGIT_CEILING * jnp.tanh(logits * scale * RECIPROCAL_HEAT / LOGIT_CEILING)
        exp_total += jnp.sum(jnp.exp(capped), -1, keepdims=True)
        begin = ((zlo * 4 + y) * 2 + (core ^ spot)) * half
        column = begin + lax.broadcasted_iota(jnp.int32, capped.shape, 1)
        picked += jnp.sum(jnp.where(column == wanted_ref[...], capped, 0.0), -1, keepdims=True)
    plane, each, lanes = out_ref.shape
    lane = lax.broadcasted_iota(jnp.int32, (plane * each, lanes), 1)
    sums = jnp.where(lane == 0, exp_total, jnp.where(lane == 1, picked, 0.0))
    for index, place in enumerate(places):
        out_ref[place] = sums[index * each : (index + 1) * each]


def finish_kernel(sums_ref, out_ref):
    total = sums_ref[0]
    for index in range(1, sums_ref.shape[0]):
        total += sums_ref[index]
    out_ref[...] = jnp.log(total[:, :1]) - total[:, 1:2]


def per_device(
    inputs, layer_gain, layer_down, layer_up, exit_norm_gain, head_weight, targets, exit_section
):
    section = lax.axis_index(SECTION)
    place = lax.axis_index(DP)
    zhi, x, zlo, y, core = (lax.axis_index(name) for name in SECTION + DP)
    micro, tokens, width = inputs.shape
    sections = lax.axis_size(SECTION)
    plane = lax.axis_size(PLANE)
    rank = layer_up.shape[1]
    own_rank = rank // plane
    exits = micro // sections
    rows = exits * tokens
    head_rows, head_columns = head_weight.shape
    where = jnp.stack([zhi, x, zlo, y, core, section, jnp.int32(width)]).astype(jnp.int32)

    head_gain = lax.dynamic_slice_in_dim(exit_norm_gain, section * head_rows, head_rows, 0)
    scaled_head = (head_weight.astype(F32) * head_gain[:, None]).astype(BF16)

    up = layer_up[0]
    features = up.shape[1]
    came = lax.all_to_all(up, PLANE, 0, 0, tiled=True).reshape(plane, own_rank, features)

    gain = lax.dynamic_slice_in_dim(layer_gain[0], place * features, features, 0)
    scaled_down = (layer_down[0].astype(F32) * gain[:, None]).astype(BF16)
    pair = jnp.concatenate([scaled_down, up.T], 1)
    lined = direct(pair, "zlo", LINE)

    half_rows = ((sections * rows, width // 2), BF16, "v")
    own_rows, other_rows, own_square, all_rows, wanted, _ = kernel_call(
        rows_kernel,
        [
            half_rows,
            half_rows,
            ((rows, 1), F32, "v"),
            ((sections * rows, width), BF16, "v"),
            ((plane * rows, 1), jnp.int32, "v"),
            ((micro,), jnp.int32, "s"),
        ],
        [where, exit_section],
        [inputs, targets],
        scratch=[pltpu.SMEM((sections,), jnp.int32)],
    )
    lined = stack([tied(piece, came)[None] for piece in lined])
    maps = direct(lined, "y", RING)

    (leaving,) = kernel_call(
        leaving_kernel, [((2, features, rank), BF16, "v")], [where], [lined]
    )
    up_came = hop(leaving, "zhi", 1)
    head_pieces = direct(tied(scaled_head, up_came), "x", RING)
    partner_rows = hop(tied(other_rows, up_came), "core", 1)

    (state,) = kernel_call(
        state_kernel, [((2 * rows, width // 2), BF16, "v")], [where], [all_rows]
    )
    state = tied(state, up_came)
    (state,) = kernel_call(
        pair_kernel, [((4 * rows, width // 2), BF16, "v")], [], [state, hop(state, "zlo", 1)]
    )
    state = [state, hop(state, "zlo", 2)]

    (copies,) = kernel_call(
        up_kernel, [((sections, own_rank, width // 2), BF16, "v")], [where], [tied(came, own_square)]
    )
    copies = tied(copies, up_came)
    up_rows = lax.all_to_all(copies, SECTION, 0, 0, tiled=True)
    up_rows = up_rows.reshape(sections * own_rank, width // 2)

    up_came = direct(tied(up_came, *maps), "y", RING)

    sums = ((2 * sections * rows + 4 * own_rank, rank), F32, "v")
    keep, send, up_stay = kernel_call(
        products_kernel,
        [sums, sums, ((plane // 2, features, rank), BF16, "v")],
        [where],
        [own_rows, partner_rows, up_rows, *maps],
    )
    (outgoing,) = kernel_call(
        combine_kernel, [((sections, 4 * rows, rank), F32, "v")], [], [keep, hop(send, "core", 1)]
    )
    line_rows = ((4 * rows, width // 2), BF16, "v")
    state = kernel_call(part_kernel, [line_rows, line_rows], [], [tied(part, send) for part in state])
    passing, staying = ring(*state, "y")

    outgoing = tied(outgoing, *up_came, *state)
    incoming = lax.all_to_all(outgoing, SECTION, 0, 0, tiled=True)
    (gram,) = kernel_call(
        gram_kernel, [((4 * own_rank, sections * rank), BF16, "v")], [], [incoming]
    )
    gram = spread(tied(gram, *passing[1:3], *staying[1:3]), "zlo")
    gram = spread(tied(gram, passing[3], staying[3]), "y").reshape(-1, sections * rank)
    head = stack([tied(piece, outgoing) for piece in head_pieces])
    other_head = hop(head, "core", 1)
    wide = 2 * head_columns
    mine, theirs = kernel_call(
        correction_kernel,
        [((rank, wide), F32, "v"), ((rank, wide), BF16, "v")],
        [where],
        [up_stay, *up_came, head, other_head],
    )
    mine = mine + hop(theirs, "core", 1).astype(F32)
    mine = (mine + hop(mine.astype(BF16), "zhi", 1).astype(F32)).astype(BF16)
    correction = direct(mine, "x", RING)

    def through(pieces, dtype):
        shape = (plane * rows, wide)
        return kernel_call(
            head_kernel, [(shape, dtype, "v")], [], [*pieces, head, other_head]
        )[0]

    passing = through(passing, BF16)
    passed = hop(passing, "zhi", 1)
    base = through(staying, F32)

    gram = tied(gram, mine, passing, staying[3])
    steps = jnp.arange(4, dtype=jnp.int32)
    at = ((steps[None, :] * 4 + steps[:, None]) * own_rank)[..., None, None]
    at = at + (steps * rank)[:, None] + jnp.arange(own_rank, dtype=jnp.int32)
    line = jnp.arange(4 * rank, dtype=jnp.int32)[:, None]
    sorting = (line == at.reshape(1, -1)).astype(BF16)
    gram = jnp.dot(sorting, gram, preferred_element_type=F32).astype(BF16)
    partner_gram = hop(gram, "core", 1)
    (latents,) = kernel_call(
        chain_kernel,
        [((rows, (sections + 1) * rank), BF16, "v")],
        [where],
        [incoming, gram, partner_gram, own_square],
        scratch=[
            pltpu.VMEM((rows, sections * rank), BF16),
            pltpu.VMEM((sections * rank, sections * rank), BF16),
        ],
    )

    latents = spread(tied(latents, passed, *correction), PLANE)
    correction = stack(correction)
    other_correction = hop(correction, "core", 1)
    (sums,) = kernel_call(
        losses_kernel,
        [((plane, rows, rank), F32, "v")],
        [where],
        [latents, correction, other_correction, base, passed, wanted],
    )
    sums = lax.all_to_all(sums, PLANE, 0, 0, tiled=True)
    (losses,) = kernel_call(finish_kernel, [((rows, 1), F32, "v")], [], [sums])
    return losses.reshape(1, exits, tokens)


def solution(mesh):
    split = Mesh(mesh.devices.reshape(2, 4, 4, 4, 2), SECTION + DP)
    placed = (
        P(None, DP, None),
        P(SECTION, None),
        P(SECTION, DP, None),
        P(SECTION, None, DP),
        P(),
        P(SECTION, DP),
        P(),
        P(),
    )
    return jax.shard_map(
        per_device, mesh=split, in_specs=placed, out_specs=P(SECTION, None, DP), check_vma=False
    )
```
